256 devices in a mesh: grp: 8 (over z_lo, core), nbr: 32 (over z_hi, y, x).
Axes of the slice: x: 4, y: 4, z: 8 (z_hi: 2, z_lo: 4; z = z_hi * 4 + z_lo), core: 2. Of those that a mesh axis runs over, the one named last changes fastest.
Arguments:
- tokens: bfloat16 [32, 448, 4096], P('nbr'), may hold values from -6 to 6
- encoded: bfloat16 [64, 128, 4096], P('nbr'), may hold values from -6 to 6
- neighbour_ids: int32 [32, 7, 2], P('nbr'), may hold values from 0 to 63, as said below
- w_query: bfloat16 [4096, 2048], P('nbr', 'grp'), may hold values from -0.09375 to 0.09375
- w_key: bfloat16 [4096, 2048], P('nbr', 'grp'), may hold values from -0.09375 to 0.09375
- w_value: bfloat16 [4096, 2048], P('nbr', 'grp'), may hold values from -0.09375 to 0.09375
- w_out: bfloat16 [2048, 4096], P('grp', 'nbr'), may hold values from -0.125 to 0.125
- d_out: bfloat16 [32, 448, 4096], P('nbr'), may hold values from -6 to 6
Outputs:
- attended: bfloat16 [32, 448, 4096], P('nbr', None, 'grp')
- d_tokens: bfloat16 [32, 448, 4096], P('nbr', None, 'grp')
- grad_query: float32 [4096, 2048], P('nbr', 'grp')
- grad_key: float32 [4096, 2048], P('nbr', 'grp')
- grad_value: float32 [4096, 2048], P('nbr', 'grp')
- grad_out: float32 [2048, 4096], P('grp', 'nbr')
The draws below stay inside these ranges and needn't reach their ends.
Inputs may be any that keep to these rules, and one draw needn't show every extreme that they name: `neighbour_ids`: within one sequence the 14 ids lie in distinct blocks of 2 consecutive entries (id // 2 differs between any two of them), and one such block is named by every sequence.
All inputs are finite; a program needn't handle non-finite values.
Results may differ from the reference program's by a relative error of at most 0.03.
Values may be sent and summed in bfloat16 or wider, within the bound.
No kernel may reach another device: no remote copies, remote signals or barrier semaphores. Data moves between devices by JAX's collectives and lax.ppermute only.
A program may use at most 128 MiB of HBM per device.

```python
import math
import jax
import jax.numpy as jnp
from jax import lax

D = 4096
HEADS = 16
HS = 128
CH = 64
NEIGH = 2
RLEN = 128
TOK_DEV = 448
E_DEV = 2
SEQS = 32
SPANS = 7
ENTRIES = 64
N_GRP = 8
N_NBR = 32


def draw_neighbour_ids(key, part):
    key = jax.random.fold_in(key, 7)
    pick_key, order_key, place_key, entry_key = jax.random.split(key, 4)
    blocks = ENTRIES // E_DEV
    wanted = SPANS * NEIGH
    shared = jax.random.randint(pick_key, (), 0, blocks)
    orders = jax.vmap(lambda sub_key: jax.random.permutation(sub_key, blocks))(jax.random.split(order_key, SEQS))
    ranking = jnp.where(orders == shared, -1, jnp.arange(blocks)[None, :])
    chosen = jnp.take_along_axis(orders, jnp.argsort(ranking, axis=1), axis=1)[:, :wanted]
    places = jax.vmap(lambda sub_key: jax.random.permutation(sub_key, wanted))(jax.random.split(place_key, SEQS))
    chosen = jnp.take_along_axis(chosen, places, axis=1)
    in_block = jax.random.randint(entry_key, (SEQS, wanted), 0, E_DEV)
    return (chosen * E_DEV + in_block).reshape(SEQS, SPANS, NEIGH).astype(jnp.int32)


def block_levels(key, extent, cuts, least, largest):
    def one(dim, parts):
        draws = jax.random.uniform(jax.random.fold_in(jax.random.fold_in(key, 6), dim), (parts,), jnp.float32, least / len(cuts), largest / len(cuts))
        return jnp.repeat(jnp.exp(draws), extent[dim] // parts).reshape((-1,) + (1,) * (len(extent) - dim - 1))

    gain = one(*cuts[0])
    for cut in cuts[1:]:
        gain = gain * one(*cut)
    return gain


def scatter_about(rng, extent, scale, limit, shards=(), kind=jnp.bfloat16):
    loudness = block_levels(rng, extent, shards, -0.22, 0.18) if shards else 1.0
    array = jax.random.normal(rng, extent, jnp.float32) * scale * loudness
    return jnp.minimum(jnp.maximum(array, -limit), limit).astype(kind)


def setup_inputs(seed: int = 0) -> dict:
    key_list = jax.random.split(jax.random.key(seed), 9)
    return {
        "tokens": scatter_about(key_list[0], (SEQS, TOK_DEV, D), 1.0, 6.0, ((0, 32),)),
        "encoded": scatter_about(key_list[1], (ENTRIES, RLEN, D), 1.0, 6.0, ((0, 32),)),
        "neighbour_ids": draw_neighbour_ids(jax.random.fold_in(key_list[8], 71), 0),
        "w_query": scatter_about(key_list[3], (D, HEADS * HS), D ** -0.5, 0.09375, ((0, 32), (1, 8))),
        "w_key": scatter_about(key_list[4], (D, HEADS * HS), D ** -0.5, 0.09375, ((0, 32), (1, 8))),
        "w_value": scatter_about(key_list[5], (D, HEADS * HS), D ** -0.5, 0.09375, ((0, 32), (1, 8))),
        "w_out": scatter_about(key_list[6], (HEADS * HS, D), (HEADS * HS) ** -0.5, 0.125, ((0, 8), (1, 32))),
        "d_out": scatter_about(key_list[7], (SEQS, TOK_DEV, D), 1.0, 6.0, ((0, 32),)),
    }


def shift_in(rows, span_len):
    filler = jnp.zeros((span_len - 1,) + rows.shape[1:], rows.dtype)
    return jnp.concatenate([rows[span_len - 1:], filler], 0)

def shift_out(rows, span_len):
    filler = jnp.zeros((span_len - 1,) + rows.shape[1:], rows.dtype)
    return jnp.concatenate([filler, rows[:rows.shape[0] - span_len + 1]], 0)

def to_low(value):
    return lax.optimization_barrier(value.astype(jnp.bfloat16)).astype(jnp.float32)

def reference(tokens, encoded, neighbour_ids, w_query, w_key, w_value, w_out, d_out):
    head_cols = HEADS * HS // N_GRP
    group_heads = head_cols // HS
    score_scale = 1.0 / math.sqrt(HS)
    seq_ids = neighbour_ids.reshape(SEQS, SPANS * NEIGH).astype(jnp.int32)
    enc_flat = encoded.reshape(ENTRIES * RLEN, D)
    attended = jnp.zeros((SEQS, TOK_DEV, D), jnp.float32)
    d_tokens = jnp.zeros((SEQS, TOK_DEV, D), jnp.float32)
    query_parts, key_parts, value_parts, out_parts = ([], [], [], [])
    contract_rows = (((0,), (0,)), ((), ()))
    contract_cols = (((1,), (1,)), ((), ()))
    for head_group in range(N_GRP):
        lower = head_group * head_cols
        wq_group = w_query[:, lower:lower + head_cols]
        wkv_group = jnp.concatenate([w_key[:, lower:lower + head_cols], w_value[:, lower:lower + head_cols]], 1)
        wo_group = w_out[lower:lower + head_cols, :]
        kv_table = jnp.dot(enc_flat, wkv_group, preferred_element_type=jnp.float32).astype(jnp.bfloat16)
        kv_table = kv_table.reshape(ENTRIES, RLEN, 2 * head_cols)

        def per_sequence(running, inputs):
            sum_query, sum_out, sum_entries = running
            rows_in, upstream, wanted = inputs
            query = jnp.dot(rows_in, wq_group, preferred_element_type=jnp.float32).astype(jnp.bfloat16)
            query_sh = shift_in(query, CH).reshape(SPANS, CH, group_heads, HS)
            fetched = kv_table[wanted].reshape(SPANS, NEIGH * RLEN, 2 * head_cols)
            key_rows = fetched[:, :, :head_cols].reshape(SPANS, NEIGH * RLEN, group_heads, HS)
            value_rows = fetched[:, :, head_cols:].reshape(SPANS, NEIGH * RLEN, group_heads, HS)
            scores = jnp.einsum('cqhe,ckhe->chqk', query_sh.astype(jnp.float32), key_rows.astype(jnp.float32)) * score_scale
            raised = jnp.exp(scores)
            attn_probs = raised / lax.optimization_barrier(jnp.sum(raised, -1, keepdims=True))
            probs_low = attn_probs.astype(jnp.bfloat16)
            context_sh = jnp.einsum('chqk,ckhe->cqhe', probs_low.astype(jnp.float32), value_rows.astype(jnp.float32))
            context = shift_out(context_sh.astype(jnp.bfloat16).reshape(TOK_DEV, head_cols), CH)
            out_part = jnp.dot(context, wo_group, preferred_element_type=jnp.float32).astype(jnp.bfloat16)
            d_context = lax.dot_general(upstream, wo_group, contract_cols, preferred_element_type=jnp.float32).astype(jnp.bfloat16)
            d_ctx_sh = shift_in(d_context, CH).reshape(SPANS, CH, group_heads, HS)
            d_probs = jnp.einsum('cqhe,ckhe->chqk', d_ctx_sh.astype(jnp.float32), value_rows.astype(jnp.float32))
            row_dot = lax.optimization_barrier(jnp.sum(attn_probs * d_probs, -1, keepdims=True))
            d_scores = (attn_probs * (d_probs - row_dot)).astype(jnp.bfloat16).astype(jnp.float32)
            grad_query_sh = jnp.einsum('chqk,ckhe->cqhe', d_scores, key_rows.astype(jnp.float32)) * score_scale
            grad_keys = jnp.einsum('chqk,cqhe->ckhe', d_scores, query_sh.astype(jnp.float32)) * score_scale
            grad_values = jnp.einsum('chqk,cqhe->ckhe', probs_low.astype(jnp.float32), d_ctx_sh.astype(jnp.float32))
            grad_used = jnp.concatenate([grad_keys.astype(jnp.bfloat16).reshape(SPANS, NEIGH * RLEN, head_cols), grad_values.astype(jnp.bfloat16).reshape(SPANS, NEIGH * RLEN, head_cols)], -1)
            grad_used = grad_used.reshape(SPANS * NEIGH, RLEN, 2 * head_cols)
            grad_query_rows = shift_out(grad_query_sh.astype(jnp.bfloat16).reshape(TOK_DEV, head_cols), CH)
            dx_part = lax.dot_general(grad_query_rows, wq_group, contract_cols, preferred_element_type=jnp.float32).astype(jnp.bfloat16)
            sum_query = sum_query + to_low(lax.dot_general(rows_in, grad_query_rows, contract_rows, preferred_element_type=jnp.float32))
            sum_out = sum_out + to_low(lax.dot_general(context, upstream, contract_rows, preferred_element_type=jnp.float32))
            sum_entries = sum_entries.at[wanted].add(grad_used.astype(jnp.float32))
            return ((sum_query, sum_out, sum_entries), (out_part, dx_part))
        start_state = (jnp.zeros((D, head_cols), jnp.float32), jnp.zeros((head_cols, D), jnp.float32), jnp.zeros((ENTRIES, RLEN, 2 * head_cols), jnp.float32))
        final_state, (out_seq, dx_seq) = lax.scan(per_sequence, start_state, (tokens, d_out, seq_ids))
        sum_query, sum_out, sum_entries = final_state
        attended = attended + out_seq.astype(jnp.float32)
        d_tokens = d_tokens + dx_seq.astype(jnp.float32)
        entry_grads = sum_entries.astype(jnp.bfloat16)

        def owner_term(pair):
            enc_block, grad_block = pair
            return lax.dot_general(enc_block, grad_block, contract_rows, preferred_element_type=jnp.float32).astype(jnp.bfloat16)
        owner_terms = lax.map(owner_term, (enc_flat.reshape(N_NBR, E_DEV * RLEN, D), entry_grads.reshape(N_NBR, E_DEV * RLEN, 2 * head_cols)))
        kv_grad = lax.optimization_barrier(jnp.sum(owner_terms.astype(jnp.float32), 0))
        query_parts.append(sum_query)
        key_parts.append(kv_grad[:, :head_cols])
        value_parts.append(kv_grad[:, head_cols:])
        out_parts.append(sum_out)
    return (attended.astype(jnp.bfloat16), d_tokens.astype(jnp.bfloat16), jnp.concatenate(query_parts, 1), jnp.concatenate(key_parts, 1), jnp.concatenate(value_parts, 1), jnp.concatenate(out_parts, 0))
```

```python
import math

import jax
import jax.numpy as jnp
from jax import lax
from jax.experimental import pallas as pl
from jax.experimental.pallas import tpu as pltpu
from jax.sharding import Mesh, PartitionSpec as P

HS = 128
CH = 64
RLEN = 128
BF = jnp.bfloat16
F32 = jnp.float32
RING = 4
VMEM_LIMIT = 48 * 1024 * 1024


def shift_perm(axis, k):
    n = lax.axis_size(axis)
    return [(i, (i + k) % n) for i in range(n)]


def fetch(value, axis, k):
    return lax.ppermute(value, axis, shift_perm(axis, -k))


def deliver(value, axis, k):
    return lax.ppermute(value, axis, shift_perm(axis, k))


def swap(value, axis, bit=1):
    n = lax.axis_size(axis)
    return lax.ppermute(value, axis, [(i, i ^ bit) for i in range(n)])


def ring_gather_direct(value, axis):
    return [value] + [fetch(value, axis, k) for k in range(1, RING)]


def ring_gather_forward(value, axis):
    half = value.shape[0] // 2
    ahead = fetch(value, axis, 1)
    behind = fetch(value, axis, -1)
    far_a = fetch(ahead[:half], axis, 1)
    far_b = fetch(behind[half:], axis, -1)
    return [value, ahead, far_a, far_b, behind]


def ring_sum(parts, axis):
    total = parts[0].astype(F32)
    for k in range(1, RING):
        total = total + deliver(parts[k], axis, k).astype(F32)
    return total


def reorder_kernel(places, src, dst):
    for j in range(src.shape[1] // 128):
        start = pl.multiple_of(places[j] * 128, 128)
        dst[:, j * 128 : (j + 1) * 128] = src[:, pl.ds(start, 128)]


def reorder(rows, places):
    return pl.pallas_call(
        reorder_kernel,
        out_shape=jax.ShapeDtypeStruct(rows.shape, rows.dtype),
        in_specs=[
            pl.BlockSpec(memory_space=pltpu.SMEM),
            pl.BlockSpec(memory_space=pltpu.VMEM),
        ],
        out_specs=pl.BlockSpec(memory_space=pltpu.VMEM),
        compiler_params=pltpu.CompilerParams(vmem_limit_bytes=VMEM_LIMIT),
        name="reorder",
    )(places, rows)


def dot_nt(a, b):
    return lax.dot_general(a, b, (((1,), (1,)), ((), ())), preferred_element_type=F32)


def dot_tn(a, b):
    return lax.dot_general(a, b, (((0,), (0,)), ((), ())), preferred_element_type=F32)


def dot_nn(a, b):
    return jnp.dot(a, b, preferred_element_type=F32)


def attention_kernel(
    pos_p, pos_q, query, d_ctx, kv_p, kv_q, context, d_query, d_kv_p, d_kv_q, ctx_f, dq_f
):
    scale = 1.0 / math.sqrt(HS)
    spans = query.shape[0] // CH
    for head, (pos, kv, d_kv) in enumerate(((pos_p, kv_p, d_kv_p), (pos_q, kv_q, d_kv_q))):
        cols = slice(head * HS, (head + 1) * HS)
        for c in range(spans):
            rows = slice(c * CH, (c + 1) * CH)
            first, second = pos[2 * c], pos[2 * c + 1]
            q = query[rows, cols]
            dc = d_ctx[rows, cols]
            keys = jnp.concatenate([kv[first, :, :HS], kv[second, :, :HS]], 0)
            values = jnp.concatenate([kv[first, :, HS:], kv[second, :, HS:]], 0)
            raised = jnp.exp(dot_nt(q, keys) * scale)
            probs = raised / jnp.sum(raised, -1, keepdims=True)
            low = probs.astype(BF)
            ctx_f[rows, cols] = dot_nn(low, values)
            d_probs = dot_nt(dc, values)
            row_dot = jnp.sum(probs * d_probs, -1, keepdims=True)
            d_scores = (probs * (d_probs - row_dot)).astype(BF)
            dq_f[rows, cols] = dot_nn(d_scores, keys) * scale
            d_keys = (dot_tn(d_scores, q) * scale).astype(BF)
            d_values = dot_tn(low, dc).astype(BF)
            d_kv[first, :, :HS] = d_keys[:RLEN]
            d_kv[first, :, HS:] = d_values[:RLEN]
            d_kv[second, :, :HS] = d_keys[RLEN:]
            d_kv[second, :, HS:] = d_values[RLEN:]
    row = lax.broadcasted_iota(jnp.int32, ctx_f.shape, 0)
    for src, dst in ((ctx_f, context), (dq_f, d_query)):
        moved = pltpu.roll(src[...], CH - 1, 0)
        dst[...] = jnp.where(row >= CH - 1, moved, 0.0).astype(BF)


def attention(pos_p, pos_q, query, d_ctx, kv_p, kv_q):
    rows = jax.ShapeDtypeStruct(query.shape, BF)
    smem = pl.BlockSpec(memory_space=pltpu.SMEM)
    vmem = pl.BlockSpec(memory_space=pltpu.VMEM)
    return pl.pallas_call(
        attention_kernel,
        out_shape=(
            rows,
            rows,
            jax.ShapeDtypeStruct(kv_p.shape, BF),
            jax.ShapeDtypeStruct(kv_q.shape, BF),
        ),
        in_specs=[smem, smem, vmem, vmem, vmem, vmem],
        out_specs=(vmem, vmem, vmem, vmem),
        scratch_shapes=[pltpu.VMEM(query.shape, F32), pltpu.VMEM(query.shape, F32)],
        compiler_params=pltpu.CompilerParams(vmem_limit_bytes=VMEM_LIMIT),
        name="attention",
    )(pos_p, pos_q, query, d_ctx, kv_p, kv_q)


def shift_in(rows):
    filler = jnp.zeros((CH - 1,) + rows.shape[1:], rows.dtype)
    return jnp.concatenate([rows[CH - 1 :], filler], 0)


def pick(flags, ones, zeros):
    return jnp.where(flags[..., None, None] == 1, ones, zeros)


def on_device(tokens, encoded, neighbour_ids, w_query, w_key, w_value, w_out, d_out):
    me_x, me_y, me_zh = lax.axis_index("x"), lax.axis_index("y"), lax.axis_index("zh")
    me_zl, me_c = lax.axis_index("zl"), lax.axis_index("c")
    k4 = jnp.arange(RING, dtype=jnp.int32)
    k2 = jnp.arange(2, dtype=jnp.int32)
    cols = w_query.shape[1]
    width = tokens.shape[2]
    chunk = width // 32

    def block_number(zh, y, x):
        return zh * 16 + y * 4 + x

    places_a = block_number(
        (me_zh ^ k2)[None, None, :],
        ((me_y + k4) % RING)[None, :, None],
        ((me_x + k4) % RING)[:, None, None],
    ).reshape(32)
    places_b = block_number(
        (me_zh ^ k2)[None, None, :],
        ((me_y + k4) % RING)[:, None, None],
        ((me_x + k4) % RING)[None, :, None],
    ).reshape(32)

    def position(zh, y, x):
        kx, ky, zr = (x - me_x) % RING, (y - me_y) % RING, zh ^ me_zh
        return kx * 8 + ky * 2 + zr, ky * 8 + kx * 2 + zr

    wanted = neighbour_ids[0].reshape(-1)
    block = wanted // 2
    pos_a, pos_b = position(block // 16, (block // 4) % 4, block % 4)
    hit = block[None, :] == jnp.arange(32, dtype=jnp.int32)[:, None]
    asking = jnp.sum(jnp.where(hit, (wanted % 2)[None, :] + 1, 0), axis=1).astype(jnp.int32)
    asked_y = jnp.stack(ring_gather_direct(asking, "y"))
    asked_x = jnp.stack(ring_gather_direct(asking, "x"))

    def local_order(asked, zr):
        flipped = jnp.where(asked > 0, ((asked - 1) ^ me_c) + 1, 0)
        return jnp.where(zr == 1, flipped, asked)

    row_blocks = block_number((me_zh ^ k2)[None, :], me_y, ((me_x + k4) % RING)[:, None])
    col_blocks = block_number((me_zh ^ k2)[None, :], ((me_y + k4) % RING)[:, None], me_x)
    asked_p = local_order(asked_y[:, row_blocks], k2[None, None, :])
    asked_q = local_order(asked_x[:, col_blocks], k2[None, None, :])

    group_a = jnp.concatenate([w_query, w_key], 1)
    group_b = jnp.concatenate([w_out.T, w_value], 1)
    both = jnp.stack([group_a, group_b])
    other = swap(both, "zh")
    shard_a = jnp.stack([both[0], other[0]])
    shard_b = jnp.stack([both[1], other[1]])
    stage_a = jnp.stack(ring_gather_direct(shard_a, "y"))
    stage_b = jnp.stack(ring_gather_direct(shard_b, "x"))
    full_a = jnp.concatenate(ring_gather_forward(stage_a, "x"), 0)
    full_b = jnp.concatenate(ring_gather_forward(stage_b, "y"), 0)
    full_a = full_a.reshape(width, 2 * cols)
    full_b = full_b.reshape(width, 2 * cols)
    wq, wk = full_a[:, :cols], full_a[:, cols:]
    wo, wv = full_b[:, :cols], full_b[:, cols:]

    far = swap(encoded[me_c], "zh")
    far_pair = swap(far, "c")
    enc_all = jnp.concatenate([encoded[0], encoded[1], far, far_pair], 0)
    enc_a = reorder(enc_all, places_a)
    enc_b = reorder(enc_all, places_b)
    tok_a = reorder(tokens[0], places_a)
    up_b = reorder(d_out[0], places_b)

    keys = dot_nn(enc_a, wk).astype(BF).reshape(2, 2, RLEN, cols)
    values = dot_nn(enc_b, wv).astype(BF).reshape(2, 2, RLEN, cols)
    table_p = jnp.concatenate([keys[..., :HS], values[..., :HS]], -1)
    table_q = jnp.concatenate([keys[..., HS:], values[..., HS:]], -1)
    row_p = jnp.stack(ring_gather_direct(table_p, "x"))
    row_q = jnp.stack(ring_gather_direct(table_q, "y"))
    send_p = [pick(asked_p[k] - 1, row_p[:, :, 1], row_p[:, :, 0]) for k in range(RING)]
    send_q = [pick(asked_q[k] - 1, row_q[:, :, 1], row_q[:, :, 0]) for k in range(RING)]
    kv_p = jnp.stack([send_p[0]] + [fetch(send_p[RING - k], "y", k) for k in range(1, RING)])
    kv_q = jnp.stack([send_q[0]] + [fetch(send_q[RING - k], "x", k) for k in range(1, RING)])
    kv_p = kv_p.reshape(32, RLEN, 2 * HS)
    kv_q = kv_q.reshape(32, RLEN, 2 * HS)

    query = shift_in(dot_nn(tok_a, wq).astype(BF))
    d_context = shift_in(dot_nn(up_b, wo).astype(BF))

    context, d_query, d_kv_p, d_kv_q = attention(pos_b, pos_a, query, d_context, kv_p, kv_q)

    def return_grads(d_kv, asked, first, second):
        parts = d_kv.reshape(RING, RING, 2, RLEN, 2 * HS)
        total = [0.0, 0.0]
        for k in range(RING):
            came = parts[0] if k == 0 else deliver(parts[k], first, k)
            flags = asked[(RING - k) % RING]
            for e in range(2):
                total[e] = total[e] + pick(
                    (flags == e + 1).astype(jnp.int32), came.astype(F32), jnp.zeros((), F32)
                )
        low = jnp.stack(total, 2).astype(BF)
        return ring_sum([low[k] for k in range(RING)], second).astype(BF)

    grads_p = return_grads(d_kv_p, asked_p, "y", "x")
    grads_q = return_grads(d_kv_q, asked_q, "x", "y")

    lr, hr = k2[None, :, None, None], k2[None, None, :, None]
    part_c = me_c ^ k2[:, None, None, None]
    part_lo, part_hi = (me_zl % 2) ^ lr, (me_zl // 2) ^ hr
    chosen_a, chosen_b = position(part_hi, 2 * part_lo + part_c, k4[None, None, None, :])
    wq_cols = wq.reshape(32, chunk, cols)[chosen_a.reshape(32)].reshape(8, 4 * chunk, cols)
    wo_cols = wo.reshape(32, chunk, cols)[chosen_b.reshape(32)].reshape(8, 4 * chunk, cols)

    def group_sum(rows, weights):
        term = jnp.einsum("te,pde->ptd", rows, weights, preferred_element_type=F32).astype(BF)
        half = (term[:4].astype(F32) + swap(term[4:], "c").astype(F32)).astype(BF)
        pair = (half[:2].astype(F32) + swap(half[2:], "zl", 1).astype(F32)).astype(BF)
        return (pair[0].astype(F32) + swap(pair[1], "zl", 2).astype(F32)).astype(BF)

    attended = group_sum(context, wo_cols)
    d_tokens = group_sum(d_query, wq_cols)

    def block_sum(term, first, second):
        parts = term.reshape(RING, RING, 2, chunk, cols)
        line = ring_sum([parts[k] for k in range(RING)], first).astype(BF)
        return ring_sum([line[k] for k in range(RING)], second).astype(BF)

    def halves_sum(a, b):
        mine = jnp.stack([a[0], b[0]]).astype(F32)
        return mine + swap(jnp.stack([a[1], b[1]]), "zh").astype(F32)

    sum_query = block_sum(dot_tn(tok_a, d_query).astype(BF), "x", "y")
    sum_out = block_sum(dot_tn(up_b, context).astype(BF), "y", "x")
    grad_query, grad_out = halves_sum(sum_query, sum_out)

    rows = 4 * RLEN
    grads_k = jnp.concatenate([grads_p[..., :HS], grads_q[..., :HS]], -1).reshape(rows, cols)
    grads_v = jnp.concatenate([grads_p[..., HS:], grads_q[..., HS:]], -1).reshape(rows, cols)
    sum_key = block_sum(dot_tn(enc_a, grads_k).astype(BF), "x", "y")
    sum_value = block_sum(dot_tn(enc_b, grads_v).astype(BF), "y", "x")
    grad_key, grad_value = halves_sum(sum_key, sum_value)

    return attended[None], d_tokens[None], grad_query, grad_key, grad_value, grad_out.T


def solution(mesh):
    grid = Mesh(mesh.devices.reshape(4, 2, 2, 4, 4), ("zl", "c", "zh", "y", "x"))
    grp, nbr = ("zl", "c"), ("zh", "y", "x")
    in_specs = (
        P(nbr, None, None),
        P(nbr, None, None),
        P(nbr, None, None),
        P(nbr, grp),
        P(nbr, grp),
        P(nbr, grp),
        P(grp, nbr),
        P(nbr, None, None),
    )
    out_specs = (
        P(nbr, None, grp),
        P(nbr, None, grp),
        P(nbr, grp),
        P(nbr, grp),
        P(nbr, grp),
        P(grp, nbr),
    )
    return jax.shard_map(
        on_device, mesh=grid, in_specs=in_specs, out_specs=out_specs, check_vma=False
    )
```

```python
import functools
import math

import jax
import jax.numpy as jnp
from jax import lax
from jax.experimental import pallas as pl
from jax.experimental.pallas import tpu as pltpu
from jax.sharding import Mesh, PartitionSpec as P

HS = 128
CH = 64
RLEN = 128
BF = jnp.bfloat16
F32 = jnp.float32
VMEM_LIMIT = 48 * 1024 * 1024


DIMS = {"xa": ("x", 1), "xb": ("x", 3), "ya": ("y", 1), "yb": ("y", 3)}
PATHS = {
    "q": ("xa", "xb", "ya", "yb"),
    "o": ("xb", "xa", "yb", "ya"),
    "k": ("ya", "yb", "xa", "xb"),
    "v": ("yb", "ya", "xb", "xa"),
}
TABLES = ("q", "o", "k", "v")


def swap(value, axis, bit=1):
    n = lax.axis_size(axis)
    return lax.ppermute(value, axis, [(i, i ^ bit) for i in range(n)])


def trade(value, dim):
    axis, bit = DIMS[dim]
    return swap(value, axis, bit)


def gate(values, *after):
    return lax.optimization_barrier((tuple(values), after))[0]


def add_low(a, b):
    return (a.astype(F32) + b.astype(F32)).astype(BF)


def places_of(path, me_zh, me_y, me_x):
    x = y = jnp.zeros((1,) * 5, jnp.int32)
    bit = jnp.arange(2, dtype=jnp.int32)
    for place, dim in enumerate(reversed(path)):
        along = bit.reshape((1,) * place + (2,) + (1,) * (4 - place))
        axis, step = DIMS[dim]
        if axis == "x":
            x = x ^ (along * step)
        else:
            y = y ^ (along * step)
    zh = bit ^ me_zh
    return (zh * 16 + (y ^ me_y) * 4 + (x ^ me_x)).reshape(32)


def position(path, block, me_zh, me_y, me_x):
    x, y, zh = (block % 4) ^ me_x, ((block // 4) % 4) ^ me_y, (block // 16) ^ me_zh
    total = zh
    for place, dim in enumerate(path):
        rel = x if DIMS[dim][0] == "x" else y
        bit = (rel // 2) if dim[1] == "b" else ((rel // 2) ^ (rel % 2))
        total = total + bit * (2 << place)
    return total


def reorder_kernel(counts, places, *refs):
    srcs, dsts = refs[: counts[0]], refs[counts[0] :]
    for which, dst in enumerate(dsts):
        for j in range(32):
            start = pl.multiple_of(places[which, j] * 128, 128)
            row = 0
            for src in srcs:
                rows = src.shape[0]
                dst[row : row + rows, j * 128 : (j + 1) * 128] = src[:, pl.ds(start, 128)]
                row += rows


def reorder(places, *rows, total=None):
    height = sum(r.shape[0] for r in rows)
    total = total or height
    block = pl.BlockSpec((height, rows[0].shape[1]), lambda i: (0, 0))
    shape = jax.ShapeDtypeStruct((total, rows[0].shape[1]), rows[0].dtype)
    return pl.pallas_call(
        functools.partial(reorder_kernel, (len(rows),)),
        out_shape=(shape,) * len(places),
        grid=(1,),
        in_specs=[pl.BlockSpec(memory_space=pltpu.SMEM)]
        + [pl.BlockSpec(r.shape, lambda i: (0, 0)) for r in rows],
        out_specs=(block,) * len(places),
        compiler_params=pltpu.CompilerParams(vmem_limit_bytes=VMEM_LIMIT),
        name="reorder",
    )(jnp.stack(places), *rows)


def reorder_far_kernel(places, first_in, second_in, far, far_pair, first, second):
    for which, dst in enumerate((first, second)):
        for j in range(32):
            start = pl.multiple_of(places[which, j] * 128, 128)
            dst[:128, j * 128 : (j + 1) * 128] = far[:, pl.ds(start, 128)]
            dst[128:, j * 128 : (j + 1) * 128] = far_pair[:, pl.ds(start, 128)]


def reorder_far(places, first, second, far, far_pair):
    shape = jax.ShapeDtypeStruct(first.shape, first.dtype)
    whole = pl.BlockSpec(memory_space=pl.ANY)
    near = pl.BlockSpec(far.shape, lambda i: (0, 0))
    half = pl.BlockSpec((first.shape[0] // 2, first.shape[1]), lambda i: (1, 0))
    return pl.pallas_call(
        reorder_far_kernel,
        grid=(1,),
        out_shape=(shape, shape),
        in_specs=[pl.BlockSpec(memory_space=pltpu.SMEM), whole, whole, near, near],
        out_specs=(half, half),
        input_output_aliases={1: 0, 2: 1},
        compiler_params=pltpu.CompilerParams(vmem_limit_bytes=VMEM_LIMIT),
        name="reorder_far",
    )(jnp.stack(places), first, second, far, far_pair)


def columns_kernel(slots, rows, stage, rest, keep, send):
    value = rows[...]
    for part in (4, 5, 6, 7, 0, 1, 2, 3):
        dst = keep if part < 4 else send
        for pair in range(2):
            weights = []
            for i in range(2):
                place = slots[part * 4 + pair * 2 + i]
                inner = place % 16
                weights.append(jnp.where(place // 16 == 0, stage[inner], rest[inner]))
            total = dot_nt(value, jnp.concatenate(weights, 0))
            dst[part % 4, :, pair * 256 : (pair + 1) * 256] = total.astype(BF)


def column_parts(slots, rows, stage, rest):
    half = jax.ShapeDtypeStruct((4, rows.shape[0], 512), BF)
    vmem = pl.BlockSpec(memory_space=pltpu.VMEM)
    return pl.pallas_call(
        columns_kernel,
        out_shape=(half, half),
        in_specs=[pl.BlockSpec(memory_space=pltpu.SMEM)] + [vmem] * 3,
        out_specs=(vmem, vmem),
        compiler_params=pltpu.CompilerParams(vmem_limit_bytes=VMEM_LIMIT),
        name="columns",
    )(slots, rows, stage.reshape(16, 128, -1), rest.reshape(16, 128, -1))


def dot_nt(a, b):
    return lax.dot_general(a, b, (((1,), (1,)), ((), ())), preferred_element_type=F32)


def dot_tn(a, b):
    return lax.dot_general(a, b, (((0,), (0,)), ((), ())), preferred_element_type=F32)


def dot_nn(a, b):
    return jnp.dot(a, b, preferred_element_type=F32)


def attention_kernel(slots, entries, query, d_ctx, *refs):
    near, next_near, far = refs[0:4], refs[4:8], refs[8:12]
    context, d_query = refs[12:14]
    d_near, d_far = refs[14:18], refs[18:22]
    ctx_f, dq_f = refs[22:24]
    scale = 1.0 / math.sqrt(HS)
    spans = query.shape[0] // CH

    def load(lane, use):
        place = slots[lane, use]
        inner = place % 16
        entry = (inner % 8) * 2 + entries[lane, use]
        mine = jnp.where(inner // 8 == 0, near[lane][entry], next_near[lane][entry])
        return jnp.where(place // 16 == 0, mine, far[lane][inner])

    def store(lane, use, value):
        place = slots[lane, use]
        side, inner = place // 16, place % 16
        d_near[lane][inner] = jnp.where(side == 0, value, d_near[lane][inner])
        d_far[lane][inner] = jnp.where(side == 1, value, d_far[lane][inner])

    heads = range(2)
    for c in range(spans):
        rows = slice(c * CH, (c + 1) * CH)
        uses = (2 * c, 2 * c + 1)
        cols = [slice(h * HS, (h + 1) * HS) for h in heads]
        q = [query[rows, cols[h]] for h in heads]
        dc = [d_ctx[rows, cols[h]] for h in heads]
        keys = [jnp.concatenate([load(h, u) for u in uses], 0) for h in heads]
        values = [jnp.concatenate([load(2 + h, u) for u in uses], 0) for h in heads]
        scores = [dot_nt(q[h], keys[h]) for h in heads]
        d_probs = [dot_nt(dc[h], values[h]) for h in heads]
        raised = [jnp.exp(scores[h] * scale) for h in heads]
        probs = [raised[h] / jnp.sum(raised[h], -1, keepdims=True) for h in heads]
        low = [probs[h].astype(BF) for h in heads]
        row_dot = [jnp.sum(probs[h] * d_probs[h], -1, keepdims=True) for h in heads]
        d_scores = [(probs[h] * (d_probs[h] - row_dot[h])).astype(BF) for h in heads]
        d_values = [dot_tn(low[h], dc[h]).astype(BF) for h in heads]
        d_keys = [(dot_tn(d_scores[h], q[h]) * scale).astype(BF) for h in heads]
        for h in heads:
            ctx_f[rows, cols[h]] = dot_nn(low[h], values[h])
            dq_f[rows, cols[h]] = dot_nn(d_scores[h], keys[h]) * scale
        for h in heads:
            for half, u in enumerate(uses):
                store(h, u, d_keys[h][half * RLEN : (half + 1) * RLEN])
                store(2 + h, u, d_values[h][half * RLEN : (half + 1) * RLEN])
    row = lax.broadcasted_iota(jnp.int32, ctx_f.shape, 0)
    for src, dst in ((ctx_f, context), (dq_f, d_query)):
        moved = pltpu.roll(src[...], CH - 1, 0)
        dst[...] = jnp.where(row >= CH - 1, moved, 0.0).astype(BF)


def attention(slots, entries, query, d_ctx, near, next_near, far):
    rows = jax.ShapeDtypeStruct(query.shape, BF)
    part = jax.ShapeDtypeStruct((16, RLEN, HS), BF)
    smem = pl.BlockSpec(memory_space=pltpu.SMEM)
    vmem = pl.BlockSpec(memory_space=pltpu.VMEM)
    out = pl.pallas_call(
        attention_kernel,
        out_shape=(rows, rows) + (part,) * 8,
        in_specs=[smem, smem] + [vmem] * 14,
        out_specs=(vmem,) * 10,
        scratch_shapes=[pltpu.VMEM(query.shape, F32), pltpu.VMEM(query.shape, F32)],
        compiler_params=pltpu.CompilerParams(vmem_limit_bytes=VMEM_LIMIT),
        name="attention",
    )(slots, entries, query, d_ctx, *near, *next_near, *far)
    return out[0], out[1], out[2:6], out[6:10]


def shift_in(rows):
    filler = jnp.zeros((CH - 1,) + rows.shape[1:], rows.dtype)
    return jnp.concatenate([rows[CH - 1 :], filler], 0)


def on_device(tokens, encoded, neighbour_ids, w_query, w_key, w_value, w_out, d_out):
    me_x, me_y, me_zh = lax.axis_index("x"), lax.axis_index("y"), lax.axis_index("zh")
    me_zl, me_c = lax.axis_index("zl"), lax.axis_index("c")
    here = (me_zh, me_y, me_x)
    bit = jnp.arange(2, dtype=jnp.int32)
    cols = w_query.shape[1]
    width = tokens.shape[2]
    chunk = width // 32
    names = ("q", "o", "k", "v")
    places = {n: places_of(PATHS[n], *here) for n in names}

    mine = jnp.stack([w_query, w_out.T, w_key, w_value])
    other = swap(mine, "zh")
    stage = {n: jnp.stack([mine[i], other[i]]) for i, n in enumerate(names)}
    encoded, ids = gate((encoded, neighbour_ids), other)
    wanted = ids[0].reshape(-1)
    note = jnp.zeros((16, cols), BF).at[0, : wanted.shape[0]].set(wanted.astype(BF))
    their_ids = {}
    for step in range(3):
        if step == 0:
            came = {}
            for n in names:
                full = jnp.concatenate([stage[n].reshape(2 * chunk, cols), note], 0)
                full = trade(full, PATHS[n][0])
                came[n] = full[: 2 * chunk].reshape(2, chunk, cols)
                their_ids[PATHS[n][0]] = full[2 * chunk, : wanted.shape[0]].astype(jnp.int32)
        else:
            came = {n: trade(stage[n], PATHS[n][step]) for n in names}
        if step == 1:
            near_rows, tokens, d_out, wanted = gate(
                (encoded.reshape(-1, width), tokens, d_out, wanted), *came.values()
            )
        stage = {n: jnp.stack([stage[n], came[n]]) for n in names}
    stage = {n: stage[n].reshape(width // 2, cols) for n in names}
    rest = {n: trade(stage[n], PATHS[n][3]) for n in names}
    half = width // 2

    asks = jnp.stack([wanted] * 4 + [their_ids[PATHS[n][3]] for n in TABLES])
    block, entry = asks // 2, asks % 2
    entries = jnp.where((block // 16) == me_zh, entry, entry ^ me_c)
    slots = jnp.stack([position(PATHS[TABLES[i % 4]], block[i], *here) for i in range(8)])
    hit = slots[:, :, None, None] == jnp.arange(16, dtype=jnp.int32)[:, None]
    hit = hit & (entries[:, :, None, None] == bit)
    asked = jnp.max(hit.astype(jnp.int32), axis=1)
    (asked,) = gate((asked == 1,))
    slots, entries = slots[:4], entries[:4]

    far = swap(encoded[me_c], "zh")
    far_pair = swap(far, "c")
    (tok_q,) = reorder([places["q"]], tokens[0])
    (up_o,) = reorder([places["o"]], d_out[0])
    kv_places = [places["k"], places["v"]]
    enc_k, enc_v = reorder(kv_places, near_rows, total=2 * near_rows.shape[0])
    enc_k, enc_v = reorder_far(kv_places, enc_k, enc_v, far, far_pair)

    def project(rows, name):
        first = dot_nn(rows[:, :half], stage[name])
        return (first + dot_nn(rows[:, half:], rest[name])).astype(BF)

    keys, values = project(enc_k, "k"), project(enc_v, "v")
    query, d_context = shift_in(project(tok_q, "q")), shift_in(project(up_o, "o"))
    tables = [
        t.reshape(2, 2, RLEN, HS)
        for t in (keys[:, :HS], keys[:, HS:], values[:, :HS], values[:, HS:])
    ]
    for step in range(3):
        came = [trade(t, PATHS[n][step]) for t, n in zip(tables, TABLES)]
        if step < 2:
            tables = [jnp.stack([t, r]) for t, r in zip(tables, came)]
    near = [t.reshape(16, RLEN, HS) for t in tables]
    next_near = [t.reshape(16, RLEN, HS) for t in came]

    def choose(lane):
        parts = []
        for i, t in enumerate((near[lane], next_near[lane])):
            pairs = t.reshape(8, 2, RLEN, HS)
            second = asked[4 + lane, 8 * i : 8 * (i + 1), 1][:, None, None]
            parts.append(jnp.where(second, pairs[:, 1], pairs[:, 0]))
        return jnp.concatenate(parts, 0)

    far_side = [trade(choose(i), PATHS[n][3]) for i, n in enumerate(TABLES)]
    context, d_query, d_near, d_far = attention(
        slots, entries, query, d_context, near, next_near, far_side
    )

    part_c = me_c ^ bit[:, None, None, None]
    part_lo = (me_zl % 2) ^ bit[None, :, None, None]
    part_hi = (me_zl // 2) ^ bit[None, None, :, None]
    x4 = jnp.arange(4, dtype=jnp.int32)[None, None, None, :]
    numbers = (part_hi * 16 + (2 * part_lo + part_c) * 4 + x4).reshape(32)

    def parts_of(rows, name):
        chosen = position(PATHS[name], numbers, *here)
        return column_parts(chosen, rows, stage[name], rest[name])

    out_keep, out_send = parts_of(context, "o")
    dx_keep, dx_send = parts_of(d_query, "q")
    out_half = add_low(out_keep, swap(out_send, "c"))
    dx_half = add_low(dx_keep, swap(dx_send, "c"))
    out_pair = add_low(out_half[:2], swap(out_half[2:], "zl", 1))
    attended = add_low(out_pair[0], swap(out_pair[1], "zl", 2))
    dx_pair = add_low(dx_half[:2], swap(dx_half[2:], "zl", 1))
    d_tokens = add_low(dx_pair[0], swap(dx_pair[1], "zl", 2))

    back = [trade(t, PATHS[n][3]) for t, n in zip(d_far, TABLES)]

    def by_entry(lane, rows):
        own, came = d_near[lane][rows].astype(F32), back[lane][rows].astype(F32)
        total = []
        for e in range(2):
            ours = asked[lane, rows, e][:, None, None]
            theirs = asked[4 + lane, rows, e][:, None, None]
            total.append(jnp.where(ours, own, 0.0) + jnp.where(theirs, came, 0.0))
        return jnp.stack(total, 1).astype(BF)

    sums = []
    for lane in range(4):
        sums.append((by_entry(lane, slice(0, 8)), by_entry(lane, slice(8, 16))))
    for step in (2, 1, 0):
        sent = [s[1] for s in sums]
        came = [trade(s, PATHS[n][step]) for s, n in zip(sent, TABLES)]
        if step == 1:
            later = came
        h = sent[0].shape[0] // 2
        if step == 0:
            sums = [add_low(s[0], r) for s, r in zip(sums, came)]
        else:
            sums = [
                (add_low(s[0][:h], r[:h]), add_low(s[0][h:], r[h:])) for s, r in zip(sums, came)
            ]
    rows = 4 * RLEN
    sums = [s.reshape(rows, HS) for s in sums]
    entry_k = jnp.concatenate(sums[:2], 1)
    entry_v = jnp.concatenate(sums[2:], 1)

    def halves(rows_in, grads):
        return (
            dot_tn(rows_in[:, :half], grads).astype(BF),
            dot_tn(rows_in[:, half:], grads).astype(BF),
        )

    def block_sum(terms, name, gates=(None,) * 4):
        keep, send = terms
        for step, wait in zip((3, 2, 1, 0), gates):
            if wait is not None:
                (send,) = gate((send,), wait)
            came = trade(send, PATHS[name][step])
            if step == 0:
                return add_low(keep, came)
            h = keep.shape[0] // 2
            keep, send = add_low(keep[:h], came[:h]), add_low(keep[h:], came[h:])

    def z_sum(a, b, *after):
        ours = [t.reshape(2, chunk, cols) for t in (a, b)]
        send = jnp.stack([t[1] for t in ours])
        if after:
            (send,) = gate((send,), *after)
        came = swap(send, "zh")
        return [t[0].astype(F32) + came[i].astype(F32) for i, t in enumerate(ours)]

    early = (tuple(later), None, None, None)
    sum_q = block_sum(halves(tok_q, d_query), "q", early)
    sum_o = block_sum(halves(up_o, context), "o", early)
    grad_query, grad_out = z_sum(sum_q, sum_o)
    late = (None, out_pair, attended, dx_pair)
    sum_k = block_sum(halves(enc_k, entry_k), "k", late)
    sum_v = block_sum(halves(enc_v, entry_v), "v", late)
    grad_key, grad_value = z_sum(sum_k, sum_v)

    return attended[None], d_tokens[None], grad_query, grad_key, grad_value, grad_out.T


def solution(mesh):
    grid = Mesh(mesh.devices.reshape(4, 2, 2, 4, 4), ("zl", "c", "zh", "y", "x"))
    grp, nbr = ("zl", "c"), ("zh", "y", "x")
    in_specs = (
        P(nbr, None, None),
        P(nbr, None, None),
        P(nbr, None, None),
        P(nbr, grp),
        P(nbr, grp),
        P(nbr, grp),
        P(grp, nbr),
        P(nbr, None, None),
    )
    out_specs = (
        P(nbr, None, grp),
        P(nbr, None, grp),
        P(nbr, grp),
        P(nbr, grp),
        P(nbr, grp),
        P(grp, nbr),
    )
    return jax.shard_map(
        on_device, mesh=grid, in_specs=in_specs, out_specs=out_specs, check_vma=False
    )
```

```python
import functools
import math

import jax
import jax.numpy as jnp
from jax import lax
from jax.experimental import pallas as pl
from jax.experimental.pallas import tpu as pltpu
from jax.sharding import Mesh, PartitionSpec as P

HS = 128
CH = 64
RLEN = 128
BF = jnp.bfloat16
F32 = jnp.float32
VMEM_LIMIT = 48 * 1024 * 1024


DIMS = {"xa": ("x", 1), "xb": ("x", 3), "ya": ("y", 1), "yb": ("y", 3)}
PATHS = {
    "q": ("xa", "xb", "ya", "yb"),
    "o": ("xb", "xa", "yb", "ya"),
    "k": ("ya", "yb", "xa", "xb"),
    "v": ("yb", "ya", "xb", "xa"),
}
TABLES = ("q", "o", "k", "v")


def swap(value, axis, bit=1):
    n = lax.axis_size(axis)
    return lax.ppermute(value, axis, [(i, i ^ bit) for i in range(n)])


def trade(value, dim):
    axis, bit = DIMS[dim]
    return swap(value, axis, bit)


def gate(values, *after):
    return lax.optimization_barrier((tuple(values), after))[0]


def add_low(a, b):
    return (a.astype(F32) + b.astype(F32)).astype(BF)


def places_of(path, me_zh, me_y, me_x):
    x = y = jnp.zeros((1,) * 5, jnp.int32)
    bit = jnp.arange(2, dtype=jnp.int32)
    for place, dim in enumerate(reversed(path)):
        along = bit.reshape((1,) * place + (2,) + (1,) * (4 - place))
        axis, step = DIMS[dim]
        if axis == "x":
            x = x ^ (along * step)
        else:
            y = y ^ (along * step)
    zh = bit ^ me_zh
    return (zh * 16 + (y ^ me_y) * 4 + (x ^ me_x)).reshape(32)


def position(path, block, me_zh, me_y, me_x):
    x, y, zh = (block % 4) ^ me_x, ((block // 4) % 4) ^ me_y, (block // 16) ^ me_zh
    total = zh
    for place, dim in enumerate(path):
        rel = x if DIMS[dim][0] == "x" else y
        bit = (rel // 2) if dim[1] == "b" else ((rel // 2) ^ (rel % 2))
        total = total + bit * (2 << place)
    return total


def whole_block(shape):
    return pl.BlockSpec(shape, lambda i: (0,) * len(shape))


def reorder_kernel(counts, places, *refs):
    srcs, dsts = refs[: counts[0]], refs[counts[0] :]
    for which, dst in enumerate(dsts):
        for j in range(32):
            start = pl.multiple_of(places[which, j] * 128, 128)
            row = 0
            for src in srcs:
                rows = src.shape[0]
                dst[row : row + rows, j * 128 : (j + 1) * 128] = src[:, pl.ds(start, 128)]
                row += rows


def reorder(places, *rows, total=None):
    height = sum(r.shape[0] for r in rows)
    total = total or height
    block = pl.BlockSpec((height, rows[0].shape[1]), lambda i: (0, 0))
    shape = jax.ShapeDtypeStruct((total, rows[0].shape[1]), rows[0].dtype)
    return pl.pallas_call(
        functools.partial(reorder_kernel, (len(rows),)),
        out_shape=(shape,) * len(places),
        grid=(1,),
        in_specs=[pl.BlockSpec(memory_space=pltpu.SMEM)]
        + [pl.BlockSpec(r.shape, lambda i: (0, 0)) for r in rows],
        out_specs=(block,) * len(places),
        compiler_params=pltpu.CompilerParams(vmem_limit_bytes=VMEM_LIMIT),
        name="reorder",
    )(jnp.stack(places), *rows)


def reorder_far_kernel(places, first_in, second_in, far, far_pair, first, second):
    for which, dst in enumerate((first, second)):
        for j in range(32):
            start = pl.multiple_of(places[which, j] * 128, 128)
            dst[:128, j * 128 : (j + 1) * 128] = far[:, pl.ds(start, 128)]
            dst[128:, j * 128 : (j + 1) * 128] = far_pair[:, pl.ds(start, 128)]


def reorder_far(places, first, second, far, far_pair):
    shape = jax.ShapeDtypeStruct(first.shape, first.dtype)
    whole = pl.BlockSpec(memory_space=pl.ANY)
    near = pl.BlockSpec(far.shape, lambda i: (0, 0))
    half = pl.BlockSpec((first.shape[0] // 2, first.shape[1]), lambda i: (1, 0))
    return pl.pallas_call(
        reorder_far_kernel,
        grid=(1,),
        out_shape=(shape, shape),
        in_specs=[pl.BlockSpec(memory_space=pltpu.SMEM), whole, whole, near, near],
        out_specs=(half, half),
        input_output_aliases={1: 0, 2: 1},
        compiler_params=pltpu.CompilerParams(vmem_limit_bytes=VMEM_LIMIT),
        name="reorder_far",
    )(jnp.stack(places), first, second, far, far_pair)


def columns_kernel(slots, rows, stage, rest, out):
    value = rows[...]
    for part in range(8):
        for pair in range(2):
            weights = []
            for i in range(2):
                place = slots[part * 4 + pair * 2 + i]
                inner = place % 16
                weights.append(jnp.where(place // 16 == 0, stage[inner], rest[inner]))
            total = dot_nt(value, jnp.concatenate(weights, 0))
            out[part, :, pair * 256 : (pair + 1) * 256] = total.astype(BF)


def column_parts(slots, rows, stage, rest):
    vmem = pl.BlockSpec(memory_space=pltpu.VMEM)
    return pl.pallas_call(
        columns_kernel,
        out_shape=jax.ShapeDtypeStruct((8, rows.shape[0], 512), BF),
        in_specs=[pl.BlockSpec(memory_space=pltpu.SMEM)] + [vmem] * 3,
        out_specs=vmem,
        compiler_params=pltpu.CompilerParams(vmem_limit_bytes=VMEM_LIMIT),
        name="columns",
    )(slots, rows, stage.reshape(16, 128, -1), rest.reshape(16, 128, -1))


def dot_nt(a, b):
    return lax.dot_general(a, b, (((1,), (1,)), ((), ())), preferred_element_type=F32)


def dot_tn(a, b):
    return lax.dot_general(a, b, (((0,), (0,)), ((), ())), preferred_element_type=F32)


def dot_nn(a, b):
    return jnp.dot(a, b, preferred_element_type=F32)


def attention_kernel(slots, entries, query, d_ctx, *refs):
    near, next_near, far = refs[0:4], refs[4:8], refs[8:12]
    context, d_query = refs[12:14]
    d_near, d_far = refs[14:18], refs[18:22]
    ctx_f, dq_f = refs[22:24]
    scale = 1.0 / math.sqrt(HS)
    spans = query.shape[0] // CH

    def load(lane, use):
        place = slots[lane, use]
        inner = place % 16
        entry = (inner % 8) * 2 + entries[lane, use]
        mine = jnp.where(inner // 8 == 0, near[lane][entry], next_near[lane][entry])
        return jnp.where(place // 16 == 0, mine, far[lane][inner])

    def store(lane, use, value):
        place = slots[lane, use]
        side, inner = place // 16, place % 16
        d_near[lane][inner] = jnp.where(side == 0, value, d_near[lane][inner])
        d_far[lane][inner] = jnp.where(side == 1, value, d_far[lane][inner])

    heads = range(2)
    for c in range(spans):
        rows = slice(c * CH, (c + 1) * CH)
        uses = (2 * c, 2 * c + 1)
        cols = [slice(h * HS, (h + 1) * HS) for h in heads]
        q = [query[rows, cols[h]] for h in heads]
        dc = [d_ctx[rows, cols[h]] for h in heads]
        keys = [jnp.concatenate([load(h, u) for u in uses], 0) for h in heads]
        values = [jnp.concatenate([load(2 + h, u) for u in uses], 0) for h in heads]
        scores = [dot_nt(q[h], keys[h]) for h in heads]
        d_probs = [dot_nt(dc[h], values[h]) for h in heads]
        raised = [jnp.exp(scores[h] * scale) for h in heads]
        probs = [raised[h] / jnp.sum(raised[h], -1, keepdims=True) for h in heads]
        low = [probs[h].astype(BF) for h in heads]
        row_dot = [jnp.sum(probs[h] * d_probs[h], -1, keepdims=True) for h in heads]
        d_scores = [(probs[h] * (d_probs[h] - row_dot[h])).astype(BF) for h in heads]
        d_values = [dot_tn(low[h], dc[h]).astype(BF) for h in heads]
        d_keys = [(dot_tn(d_scores[h], q[h]) * scale).astype(BF) for h in heads]
        for h in heads:
            ctx_f[rows, cols[h]] = dot_nn(low[h], values[h])
            dq_f[rows, cols[h]] = dot_nn(d_scores[h], keys[h]) * scale
        for h in heads:
            for half, u in enumerate(uses):
                store(h, u, d_keys[h][half * RLEN : (half + 1) * RLEN])
                store(2 + h, u, d_values[h][half * RLEN : (half + 1) * RLEN])
    row = lax.broadcasted_iota(jnp.int32, ctx_f.shape, 0)
    for src, dst in ((ctx_f, context), (dq_f, d_query)):
        moved = pltpu.roll(src[...], CH - 1, 0)
        dst[...] = jnp.where(row >= CH - 1, moved, 0.0).astype(BF)


def attention(slots, entries, query, d_ctx, near, next_near, far):
    rows = jax.ShapeDtypeStruct(query.shape, BF)
    part = jax.ShapeDtypeStruct((16, RLEN, HS), BF)
    smem = pl.BlockSpec(memory_space=pltpu.SMEM)
    vmem = pl.BlockSpec(memory_space=pltpu.VMEM)
    ins = [query, d_ctx, *near, *next_near, *far]
    out = pl.pallas_call(
        attention_kernel,
        out_shape=(rows, rows) + (part,) * 8,
        in_specs=[smem, smem] + [vmem] * len(ins),
        out_specs=(vmem,) * 10,
        scratch_shapes=[pltpu.VMEM(query.shape, F32), pltpu.VMEM(query.shape, F32)],
        compiler_params=pltpu.CompilerParams(vmem_limit_bytes=VMEM_LIMIT),
        name="attention",
    )(slots, entries, *ins)
    return out[0], out[1], out[2:6], out[6:10]


def shift_in(rows):
    filler = jnp.zeros((CH - 1,) + rows.shape[1:], rows.dtype)
    return jnp.concatenate([rows[CH - 1 :], filler], 0)


def on_device(tokens, encoded, neighbour_ids, w_query, w_key, w_value, w_out, d_out):
    me_x, me_y, me_zh = lax.axis_index("x"), lax.axis_index("y"), lax.axis_index("zh")
    me_c = lax.axis_index("c")
    here = (me_zh, me_y, me_x)
    bit = jnp.arange(2, dtype=jnp.int32)
    cols = w_query.shape[1]
    width = tokens.shape[2]
    chunk = width // 32
    names = ("q", "o", "k", "v")
    places = {n: places_of(PATHS[n], *here) for n in names}

    mine = jnp.stack([w_query, w_out.T, w_key, w_value])
    (ids,) = gate((neighbour_ids,), mine)
    wanted = ids[0].reshape(-1)
    their_ids = [trade(wanted, PATHS[n][3]) for n in TABLES]
    other = swap(mine, "zh")
    stage = {n: jnp.stack([mine[i], other[i]]) for i, n in enumerate(names)}
    (encoded,) = gate((encoded,), other)
    for step in range(3):
        came = {n: trade(stage[n], PATHS[n][step]) for n in names}
        stage = {n: jnp.stack([stage[n], came[n]]) for n in names}
    stage = {n: stage[n].reshape(width // 2, cols) for n in names}
    rest = {n: trade(stage[n], PATHS[n][3]) for n in names}
    half = width // 2

    asks = jnp.stack([wanted] * 4 + their_ids)
    block, entry = asks // 2, asks % 2
    entries = jnp.where((block // 16) == me_zh, entry, entry ^ me_c)
    slots = jnp.stack([position(PATHS[TABLES[i % 4]], block[i], *here) for i in range(8)])
    hit = slots[:, :, None, None] == jnp.arange(16, dtype=jnp.int32)[:, None]
    hit = hit & (entries[:, :, None, None] == bit)
    asked = jnp.max(hit.astype(jnp.int32), axis=1)
    (asked,) = gate((asked == 1,))
    slots, entries = slots[:4], entries[:4]

    far = swap(encoded[me_c], "zh")
    tokens, d_out = gate((tokens, d_out), rest["k"])
    far_pair = swap(far, "c")
    (tok_q,) = reorder([places["q"]], tokens[0])
    (up_o,) = reorder([places["o"]], d_out[0])
    near_rows = encoded.reshape(-1, width)
    kv_places = [places["k"], places["v"]]
    enc_k, enc_v = reorder(kv_places, near_rows, total=2 * near_rows.shape[0])
    enc_k, enc_v = reorder_far(kv_places, enc_k, enc_v, far, far_pair)

    def project(rows, name):
        first = dot_nn(rows[:, :half], stage[name])
        return (first + dot_nn(rows[:, half:], rest[name])).astype(BF)

    keys, values = project(enc_k, "k"), project(enc_v, "v")
    query, d_context = shift_in(project(tok_q, "q")), shift_in(project(up_o, "o"))
    tables = [
        t.reshape(2, 2, RLEN, HS)
        for t in (keys[:, :HS], keys[:, HS:], values[:, :HS], values[:, HS:])
    ]
    for step in range(3):
        came = [trade(t, PATHS[n][step]) for t, n in zip(tables, TABLES)]
        if step < 2:
            tables = [jnp.stack([t, r]) for t, r in zip(tables, came)]
    near = [t.reshape(16, RLEN, HS) for t in tables]
    next_near = [t.reshape(16, RLEN, HS) for t in came]

    def choose(lane):
        parts = []
        for i, t in enumerate((near[lane], next_near[lane])):
            pairs = t.reshape(8, 2, RLEN, HS)
            second = asked[4 + lane, 8 * i : 8 * (i + 1), 1][:, None, None]
            parts.append(jnp.where(second, pairs[:, 1], pairs[:, 0]))
        return jnp.concatenate(parts, 0)

    far_side = [trade(choose(i), PATHS[n][3]) for i, n in enumerate(TABLES)]
    context, d_query, d_near, d_far = attention(
        slots, entries, query, d_context, near, next_near, far_side
    )

    numbers = jnp.arange(32, dtype=jnp.int32)

    def group_sum(rows, name):
        parts = column_parts(position(PATHS[name], numbers, *here), rows, stage[name], rest[name])
        return lax.psum_scatter(parts, ("zl", "c"), scatter_dimension=0, tiled=False)

    attended, d_tokens = group_sum(context, "o"), group_sum(d_query, "q")

    back = [trade(t, PATHS[n][3]) for t, n in zip(d_far, TABLES)]

    def by_entry(lane, rows):
        own, came = d_near[lane][rows].astype(F32), back[lane][rows].astype(F32)
        total = []
        for e in range(2):
            ours = asked[lane, rows, e][:, None, None]
            theirs = asked[4 + lane, rows, e][:, None, None]
            total.append(jnp.where(ours, own, 0.0) + jnp.where(theirs, came, 0.0))
        return jnp.stack(total, 1).astype(BF)

    sums = []
    for lane in range(4):
        sums.append((by_entry(lane, slice(0, 8)), by_entry(lane, slice(8, 16))))
    for step in (2, 1, 0):
        sent = [s[1] for s in sums]
        came = [trade(s, PATHS[n][step]) for s, n in zip(sent, TABLES)]
        if step == 2:
            second = came
        h = sent[0].shape[0] // 2
        if step == 0:
            sums = [add_low(s[0], r) for s, r in zip(sums, came)]
        else:
            sums = [
                (add_low(s[0][:h], r[:h]), add_low(s[0][h:], r[h:])) for s, r in zip(sums, came)
            ]
    rows = 4 * RLEN
    sums = [s.reshape(rows, HS) for s in sums]
    entry_k = jnp.concatenate(sums[:2], 1)
    entry_v = jnp.concatenate(sums[2:], 1)

    def halves(rows_in, grads):
        return (
            dot_tn(rows_in[:, :half], grads).astype(BF),
            dot_tn(rows_in[:, half:], grads).astype(BF),
        )

    def block_sum(terms, name, gates=(None,) * 4):
        keep, send = terms
        for step, wait in zip((3, 2, 1, 0), gates):
            if wait is not None:
                (send,) = gate((send,), wait)
            came = trade(send, PATHS[name][step])
            if step == 0:
                return add_low(keep, came)
            h = keep.shape[0] // 2
            keep, send = add_low(keep[:h], came[:h]), add_low(keep[h:], came[h:])

    def z_sum(a, b, *after):
        ours = [t.reshape(2, chunk, cols) for t in (a, b)]
        send = jnp.stack([t[1] for t in ours])
        if after:
            (send,) = gate((send,), *after)
        came = swap(send, "zh")
        return [t[0].astype(F32) + came[i].astype(F32) for i, t in enumerate(ours)]

    tok_q, up_o = gate((tok_q, up_o), *second)
    early = (tuple(sums), None, None, None)
    sum_q = block_sum(halves(tok_q, d_query), "q", early)
    sum_o = block_sum(halves(up_o, context), "o", early)
    grad_query, grad_out = z_sum(sum_q, sum_o)
    sum_k = block_sum(halves(enc_k, entry_k), "k")
    sum_v = block_sum(halves(enc_v, entry_v), "v")
    grad_key, grad_value = z_sum(sum_k, sum_v)

    return attended[None], d_tokens[None], grad_query, grad_key, grad_value, grad_out.T


def solution(mesh):
    grid = Mesh(mesh.devices.reshape(4, 2, 2, 4, 4), ("zl", "c", "zh", "y", "x"))
    grp, nbr = ("zl", "c"), ("zh", "y", "x")
    in_specs = (
        P(nbr, None, None),
        P(nbr, None, None),
        P(nbr, None, None),
        P(nbr, grp),
        P(nbr, grp),
        P(nbr, grp),
        P(grp, nbr),
        P(nbr, None, None),
    )
    out_specs = (
        P(nbr, None, grp),
        P(nbr, None, grp),
        P(nbr, grp),
        P(nbr, grp),
        P(nbr, grp),
        P(grp, nbr),
    )
    return jax.shard_map(
        on_device, mesh=grid, in_specs=in_specs, out_specs=out_specs, check_vma=False
    )
```

```python
import functools
import math

import jax
import jax.numpy as jnp
from jax import lax
from jax.experimental import pallas as pl
from jax.experimental.pallas import tpu as pltpu
from jax.sharding import Mesh, PartitionSpec as P

HS = 128
CH = 64
RLEN = 128
BF = jnp.bfloat16
F32 = jnp.float32
VMEM_LIMIT = 48 * 1024 * 1024


DIMS = {"xa": ("x", 1), "xb": ("x", 3), "ya": ("y", 1), "yb": ("y", 3)}
PATHS = {
    "q": ("xa", "xb", "ya", "yb"),
    "o": ("xb", "xa", "yb", "ya"),
    "k": ("ya", "yb", "xa", "xb"),
    "v": ("yb", "ya", "xb", "xa"),
}
TABLES = ("q", "o", "k", "v")


def swap(value, axis, bit=1):
    n = lax.axis_size(axis)
    return lax.ppermute(value, axis, [(i, i ^ bit) for i in range(n)])


def trade(value, dim):
    axis, bit = DIMS[dim]
    return swap(value, axis, bit)


def gate(values, *after):
    return lax.optimization_barrier((tuple(values), after))[0]


def add_low(a, b):
    return (a.astype(F32) + b.astype(F32)).astype(BF)


def places_of(path, me_zh, me_y, me_x):
    x = y = jnp.zeros((1,) * 5, jnp.int32)
    bit = jnp.arange(2, dtype=jnp.int32)
    for place, dim in enumerate(reversed(path)):
        along = bit.reshape((1,) * place + (2,) + (1,) * (4 - place))
        axis, step = DIMS[dim]
        if axis == "x":
            x = x ^ (along * step)
        else:
            y = y ^ (along * step)
    zh = bit ^ me_zh
    return (zh * 16 + (y ^ me_y) * 4 + (x ^ me_x)).reshape(32)


def position(path, block, me_zh, me_y, me_x):
    x, y, zh = (block % 4) ^ me_x, ((block // 4) % 4) ^ me_y, (block // 16) ^ me_zh
    total = zh
    for place, dim in enumerate(path):
        rel = x if DIMS[dim][0] == "x" else y
        bit = (rel // 2) if dim[1] == "b" else ((rel // 2) ^ (rel % 2))
        total = total + bit * (2 << place)
    return total


def whole_block(shape):
    return pl.BlockSpec(shape, lambda i: (0,) * len(shape))


def reorder_kernel(counts, places, *refs):
    srcs, dsts = refs[: counts[0]], refs[counts[0] :]
    for which, dst in enumerate(dsts):
        for j in range(32):
            start = pl.multiple_of(places[which, j] * 128, 128)
            row = 0
            for src in srcs:
                rows = src.shape[0]
                dst[row : row + rows, j * 128 : (j + 1) * 128] = src[:, pl.ds(start, 128)]
                row += rows


def reorder(places, *rows, total=None):
    height = sum(r.shape[0] for r in rows)
    total = total or height
    block = pl.BlockSpec((height, rows[0].shape[1]), lambda i: (0, 0))
    shape = jax.ShapeDtypeStruct((total, rows[0].shape[1]), rows[0].dtype)
    return pl.pallas_call(
        functools.partial(reorder_kernel, (len(rows),)),
        out_shape=(shape,) * len(places),
        grid=(1,),
        in_specs=[pl.BlockSpec(memory_space=pltpu.SMEM)]
        + [pl.BlockSpec(r.shape, lambda i: (0, 0)) for r in rows],
        out_specs=(block,) * len(places),
        compiler_params=pltpu.CompilerParams(vmem_limit_bytes=VMEM_LIMIT),
        name="reorder",
    )(jnp.stack(places), *rows)


def reorder_far_kernel(places, first_in, second_in, far, far_pair, first, second):
    for which, dst in enumerate((first, second)):
        for j in range(32):
            start = pl.multiple_of(places[which, j] * 128, 128)
            dst[:128, j * 128 : (j + 1) * 128] = far[:, pl.ds(start, 128)]
            dst[128:, j * 128 : (j + 1) * 128] = far_pair[:, pl.ds(start, 128)]


def reorder_far(places, first, second, far, far_pair):
    shape = jax.ShapeDtypeStruct(first.shape, first.dtype)
    whole = pl.BlockSpec(memory_space=pl.ANY)
    near = pl.BlockSpec(far.shape, lambda i: (0, 0))
    half = pl.BlockSpec((first.shape[0] // 2, first.shape[1]), lambda i: (1, 0))
    return pl.pallas_call(
        reorder_far_kernel,
        grid=(1,),
        out_shape=(shape, shape),
        in_specs=[pl.BlockSpec(memory_space=pltpu.SMEM), whole, whole, near, near],
        out_specs=(half, half),
        input_output_aliases={1: 0, 2: 1},
        compiler_params=pltpu.CompilerParams(vmem_limit_bytes=VMEM_LIMIT),
        name="reorder_far",
    )(jnp.stack(places), first, second, far, far_pair)


def columns_kernel(slots, rows, stage, rest, out):
    value = rows[...]
    for part in range(8):
        for pair in range(2):
            weights = []
            for i in range(2):
                place = slots[part * 4 + pair * 2 + i]
                inner = place % 16
                weights.append(jnp.where(place // 16 == 0, stage[inner], rest[inner]))
            total = dot_nt(value, jnp.concatenate(weights, 0))
            out[part, :, pair * 256 : (pair + 1) * 256] = total.astype(BF)


def column_parts(slots, rows, stage, rest):
    vmem = pl.BlockSpec(memory_space=pltpu.VMEM)
    return pl.pallas_call(
        columns_kernel,
        out_shape=jax.ShapeDtypeStruct((8, rows.shape[0], 512), BF),
        in_specs=[pl.BlockSpec(memory_space=pltpu.SMEM)] + [vmem] * 3,
        out_specs=vmem,
        compiler_params=pltpu.CompilerParams(vmem_limit_bytes=VMEM_LIMIT),
        name="columns",
    )(slots, rows, stage.reshape(16, 128, -1), rest.reshape(16, 128, -1))


def dot_nt(a, b):
    return lax.dot_general(a, b, (((1,), (1,)), ((), ())), preferred_element_type=F32)


def dot_tn(a, b):
    return lax.dot_general(a, b, (((0,), (0,)), ((), ())), preferred_element_type=F32)


def dot_nn(a, b):
    return jnp.dot(a, b, preferred_element_type=F32)


def attention_kernel(slots, entries, query, d_ctx, *refs):
    near, next_near, far = refs[0:4], refs[4:8], refs[8:12]
    context, d_query = refs[12:14]
    d_near, d_sent = refs[14:18], refs[18:22]
    ctx_f, dq_f = refs[22:24]
    d_far, sems = refs[24:28], refs[28]
    scale = 1.0 / math.sqrt(HS)
    spans = query.shape[0] // CH

    def load(lane, use):
        place = slots[lane, use]
        inner = place % 16
        entry = (inner % 8) * 2 + entries[lane, use]
        mine = jnp.where(inner // 8 == 0, near[lane][entry], next_near[lane][entry])
        return jnp.where(place // 16 == 0, mine, far[lane][inner])

    def store(lane, use, value):
        place = slots[lane, use]
        side, inner = place // 16, place % 16
        d_near[lane][inner] = jnp.where(side == 0, value, d_near[lane][inner])
        d_far[lane][inner] = jnp.where(side == 1, value, d_far[lane][inner])

    heads = range(2)
    for c in range(spans):
        rows = slice(c * CH, (c + 1) * CH)
        uses = (2 * c, 2 * c + 1)
        cols = [slice(h * HS, (h + 1) * HS) for h in heads]
        q = [query[rows, cols[h]] for h in heads]
        dc = [d_ctx[rows, cols[h]] for h in heads]
        keys = [jnp.concatenate([load(h, u) for u in uses], 0) for h in heads]
        values = [jnp.concatenate([load(2 + h, u) for u in uses], 0) for h in heads]
        scores = [dot_nt(q[h], keys[h]) for h in heads]
        d_probs = [dot_nt(dc[h], values[h]) for h in heads]
        raised = [jnp.exp(scores[h] * scale) for h in heads]
        probs = [raised[h] / jnp.sum(raised[h], -1, keepdims=True) for h in heads]
        low = [probs[h].astype(BF) for h in heads]
        row_dot = [jnp.sum(probs[h] * d_probs[h], -1, keepdims=True) for h in heads]
        d_scores = [(probs[h] * (d_probs[h] - row_dot[h])).astype(BF) for h in heads]
        d_values = [dot_tn(low[h], dc[h]).astype(BF) for h in heads]
        d_keys = [(dot_tn(d_scores[h], q[h]) * scale).astype(BF) for h in heads]
        for h in heads:
            ctx_f[rows, cols[h]] = dot_nn(low[h], values[h])
            dq_f[rows, cols[h]] = dot_nn(d_scores[h], keys[h]) * scale
        for h in heads:
            for half, u in enumerate(uses):
                store(h, u, d_keys[h][half * RLEN : (half + 1) * RLEN])
                store(2 + h, u, d_values[h][half * RLEN : (half + 1) * RLEN])
    copies = [pltpu.make_async_copy(d_far[i], d_sent[i], sems.at[i]) for i in range(4)]
    for copy in copies:
        copy.start()
    row = lax.broadcasted_iota(jnp.int32, ctx_f.shape, 0)
    for src, dst in ((ctx_f, context), (dq_f, d_query)):
        moved = pltpu.roll(src[...], CH - 1, 0)
        dst[...] = jnp.where(row >= CH - 1, moved, 0.0).astype(BF)
    for copy in copies:
        copy.wait()


def attention(slots, entries, query, d_ctx, near, next_near, far):
    rows = jax.ShapeDtypeStruct(query.shape, BF)
    part = jax.ShapeDtypeStruct((16, RLEN, HS), BF)
    smem = pl.BlockSpec(memory_space=pltpu.SMEM)
    vmem = pl.BlockSpec(memory_space=pltpu.VMEM)
    ins = [query, d_ctx, *near, *next_near, *far]
    out = pl.pallas_call(
        attention_kernel,
        out_shape=(rows, rows) + (part,) * 8,
        in_specs=[smem, smem] + [vmem] * len(ins),
        out_specs=(vmem,) * 6 + (pl.BlockSpec(memory_space=pltpu.HBM),) * 4,
        scratch_shapes=[pltpu.VMEM(query.shape, F32), pltpu.VMEM(query.shape, F32)]
        + [pltpu.VMEM(part.shape, BF)] * 4
        + [pltpu.SemaphoreType.DMA((4,))],
        compiler_params=pltpu.CompilerParams(vmem_limit_bytes=VMEM_LIMIT),
        name="attention",
    )(slots, entries, *ins)
    return out[0], out[1], out[2:6], out[6:10]


def shift_in(rows):
    filler = jnp.zeros((CH - 1,) + rows.shape[1:], rows.dtype)
    return jnp.concatenate([rows[CH - 1 :], filler], 0)


def on_device(tokens, encoded, neighbour_ids, w_query, w_key, w_value, w_out, d_out):
    me_x, me_y, me_zh = lax.axis_index("x"), lax.axis_index("y"), lax.axis_index("zh")
    me_c = lax.axis_index("c")
    here = (me_zh, me_y, me_x)
    bit = jnp.arange(2, dtype=jnp.int32)
    cols = w_query.shape[1]
    width = tokens.shape[2]
    chunk = width // 32
    names = ("q", "o", "k", "v")
    places = {n: places_of(PATHS[n], *here) for n in names}

    mine = jnp.stack([w_query, w_out.T, w_key, w_value])
    (ids,) = gate((neighbour_ids,), mine)
    wanted = ids[0].reshape(-1)
    their_ids = [trade(wanted, PATHS[n][3]) for n in TABLES]
    other = swap(mine, "zh")
    stage = {n: jnp.stack([mine[i], other[i]]) for i, n in enumerate(names)}
    (encoded,) = gate((encoded,), other)
    for step in range(3):
        came = {n: trade(stage[n], PATHS[n][step]) for n in names}
        if step == 1:
            near_rows, tokens, d_out = gate(
                (encoded.reshape(-1, width), tokens, d_out), *came.values()
            )
        if step >= 1:
            came = dict(zip(names, gate([came[n] for n in names])))
        stage = {n: jnp.stack([stage[n], came[n]]) for n in names}
    stage = {n: stage[n].reshape(width // 2, cols) for n in names}
    rest = {n: trade(stage[n], PATHS[n][3]) for n in names}
    half = width // 2

    asks = jnp.stack([wanted] * 4 + their_ids)
    block, entry = asks // 2, asks % 2
    entries = jnp.where((block // 16) == me_zh, entry, entry ^ me_c)
    slots = jnp.stack([position(PATHS[TABLES[i % 4]], block[i], *here) for i in range(8)])
    hit = slots[:, :, None, None] == jnp.arange(16, dtype=jnp.int32)[:, None]
    hit = hit & (entries[:, :, None, None] == bit)
    asked = jnp.max(hit.astype(jnp.int32), axis=1)
    (asked,) = gate((asked == 1,))
    slots, entries = slots[:4], entries[:4]

    far = swap(encoded[me_c], "zh")
    far_pair = swap(far, "c")
    (tok_q,) = reorder([places["q"]], tokens[0])
    (up_o,) = reorder([places["o"]], d_out[0])
    kv_places = [places["k"], places["v"]]
    enc_k, enc_v = reorder(kv_places, near_rows, total=2 * near_rows.shape[0])
    enc_k, enc_v = reorder_far(kv_places, enc_k, enc_v, far, far_pair)

    def project(rows, name):
        first = dot_nn(rows[:, :half], stage[name])
        return (first + dot_nn(rows[:, half:], rest[name])).astype(BF)

    keys, values = project(enc_k, "k"), project(enc_v, "v")
    query, d_context = shift_in(project(tok_q, "q")), shift_in(project(up_o, "o"))
    tables = [
        t.reshape(2, 2, RLEN, HS)
        for t in (keys[:, :HS], keys[:, HS:], values[:, :HS], values[:, HS:])
    ]
    for step in range(3):
        came = [trade(t, PATHS[n][step]) for t, n in zip(tables, TABLES)]
        if step < 2:
            tables = [jnp.stack([t, r]) for t, r in zip(tables, came)]
    near = [t.reshape(16, RLEN, HS) for t in tables]
    next_near = [t.reshape(16, RLEN, HS) for t in came]

    def choose(lane):
        parts = []
        for i, t in enumerate((near[lane], next_near[lane])):
            pairs = t.reshape(8, 2, RLEN, HS)
            second = asked[4 + lane, 8 * i : 8 * (i + 1), 1][:, None, None]
            parts.append(jnp.where(second, pairs[:, 1], pairs[:, 0]))
        return jnp.concatenate(parts, 0)

    far_side = [trade(choose(i), PATHS[n][3]) for i, n in enumerate(TABLES)]
    context, d_query, d_near, d_far = attention(
        slots, entries, query, d_context, near, next_near, far_side
    )

    numbers = jnp.arange(32, dtype=jnp.int32)

    def group_sum(rows, name):
        parts = column_parts(position(PATHS[name], numbers, *here), rows, stage[name], rest[name])
        return lax.psum_scatter(parts, ("zl", "c"), scatter_dimension=0, tiled=False)

    attended, d_tokens = group_sum(context, "o"), group_sum(d_query, "q")

    back = [trade(t, PATHS[n][3]) for t, n in zip(d_far, TABLES)]

    def by_entry(lane, rows):
        own, came = d_near[lane][rows].astype(F32), back[lane][rows].astype(F32)
        total = []
        for e in range(2):
            ours = asked[lane, rows, e][:, None, None]
            theirs = asked[4 + lane, rows, e][:, None, None]
            total.append(jnp.where(ours, own, 0.0) + jnp.where(theirs, came, 0.0))
        return jnp.stack(total, 1).astype(BF)

    sums = []
    for lane in range(4):
        sums.append((by_entry(lane, slice(0, 8)), by_entry(lane, slice(8, 16))))
    for step in (2, 1, 0):
        sent = [s[1] for s in sums]
        came = [trade(s, PATHS[n][step]) for s, n in zip(sent, TABLES)]
        h = sent[0].shape[0] // 2
        if step == 0:
            sums = [add_low(s[0], r) for s, r in zip(sums, came)]
        else:
            sums = [
                (add_low(s[0][:h], r[:h]), add_low(s[0][h:], r[h:])) for s, r in zip(sums, came)
            ]
    rows = 4 * RLEN
    sums = [s.reshape(rows, HS) for s in sums]
    entry_k = jnp.concatenate(sums[:2], 1)
    entry_v = jnp.concatenate(sums[2:], 1)

    def halves(rows_in, grads):
        return (
            dot_tn(rows_in[:, :half], grads).astype(BF),
            dot_tn(rows_in[:, half:], grads).astype(BF),
        )

    def block_sum(terms, name, gates=(None,) * 4):
        keep, send = terms
        for step, wait in zip((3, 2, 1, 0), gates):
            if wait is not None:
                (send,) = gate((send,), wait)
            came = trade(send, PATHS[name][step])
            if step == 0:
                return add_low(keep, came)
            h = keep.shape[0] // 2
            keep, send = add_low(keep[:h], came[:h]), add_low(keep[h:], came[h:])

    def z_sum(a, b, *after):
        ours = [t.reshape(2, chunk, cols) for t in (a, b)]
        send = jnp.stack([t[1] for t in ours])
        if after:
            (send,) = gate((send,), *after)
        came = swap(send, "zh")
        return [t[0].astype(F32) + came[i].astype(F32) for i, t in enumerate(ours)]

    tok_q, up_o = gate((tok_q, up_o), *sums)
    sum_q = block_sum(halves(tok_q, d_query), "q")
    sum_o = block_sum(halves(up_o, context), "o")
    grad_query, grad_out = z_sum(sum_q, sum_o)
    sum_k = block_sum(halves(enc_k, entry_k), "k")
    sum_v = block_sum(halves(enc_v, entry_v), "v")
    grad_key, grad_value = z_sum(sum_k, sum_v)

    return attended[None], d_tokens[None], grad_query, grad_key, grad_value, grad_out.T


def solution(mesh):
    grid = Mesh(mesh.devices.reshape(4, 2, 2, 4, 4), ("zl", "c", "zh", "y", "x"))
    grp, nbr = ("zl", "c"), ("zh", "y", "x")
    in_specs = (
        P(nbr, None, None),
        P(nbr, None, None),
        P(nbr, None, None),
        P(nbr, grp),
        P(nbr, grp),
        P(nbr, grp),
        P(grp, nbr),
        P(nbr, None, None),
    )
    out_specs = (
        P(nbr, None, grp),
        P(nbr, None, grp),
        P(nbr, grp),
        P(nbr, grp),
        P(nbr, grp),
        P(grp, nbr),
    )
    return jax.shard_map(
        on_device, mesh=grid, in_specs=in_specs, out_specs=out_specs, check_vma=False
    )
```

```python
import functools
import math

import jax
import jax.numpy as jnp
from jax import lax
from jax.experimental import pallas as pl
from jax.experimental.pallas import tpu as pltpu
from jax.sharding import Mesh, PartitionSpec as P

HS = 128
CH = 64
RLEN = 128
BF = jnp.bfloat16
F32 = jnp.float32
VMEM_LIMIT = 48 * 1024 * 1024


DIMS = {"xa": ("x", 1), "xb": ("x", 3), "ya": ("y", 1), "yb": ("y", 3)}
PATHS = {
    "q": ("xa", "xb", "ya", "yb"),
    "o": ("xb", "xa", "yb", "ya"),
    "k": ("ya", "yb", "xa", "xb"),
    "v": ("yb", "ya", "xb", "xa"),
}
TABLES = ("q", "o", "k", "v")


def swap(value, axis, bit=1):
    n = lax.axis_size(axis)
    return lax.ppermute(value, axis, [(i, i ^ bit) for i in range(n)])


def trade(value, dim):
    axis, bit = DIMS[dim]
    return swap(value, axis, bit)


def gate(values, *after):
    return lax.optimization_barrier((tuple(values), after))[0]


def add_low(a, b):
    return (a.astype(F32) + b.astype(F32)).astype(BF)


def places_of(path, me_zh, me_y, me_x):
    x = y = jnp.zeros((1,) * 5, jnp.int32)
    bit = jnp.arange(2, dtype=jnp.int32)
    for place, dim in enumerate(reversed(path)):
        along = bit.reshape((1,) * place + (2,) + (1,) * (4 - place))
        axis, step = DIMS[dim]
        if axis == "x":
            x = x ^ (along * step)
        else:
            y = y ^ (along * step)
    zh = bit ^ me_zh
    return (zh * 16 + (y ^ me_y) * 4 + (x ^ me_x)).reshape(32)


def position(path, block, me_zh, me_y, me_x):
    x, y, zh = (block % 4) ^ me_x, ((block // 4) % 4) ^ me_y, (block // 16) ^ me_zh
    total = zh
    for place, dim in enumerate(path):
        rel = x if DIMS[dim][0] == "x" else y
        bit = (rel // 2) if dim[1] == "b" else ((rel // 2) ^ (rel % 2))
        total = total + bit * (2 << place)
    return total


def whole_block(shape):
    return pl.BlockSpec(shape, lambda i: (0,) * len(shape))


def reorder_kernel(counts, places, *refs):
    srcs, dsts = refs[: counts[0]], refs[counts[0] :]
    for which, dst in enumerate(dsts):
        for j in range(32):
            start = pl.multiple_of(places[which, j] * 128, 128)
            row = 0
            for src in srcs:
                rows = src.shape[0]
                dst[row : row + rows, j * 128 : (j + 1) * 128] = src[:, pl.ds(start, 128)]
                row += rows


def reorder(places, *rows, total=None):
    height = sum(r.shape[0] for r in rows)
    total = total or height
    block = pl.BlockSpec((height, rows[0].shape[1]), lambda i: (0, 0))
    shape = jax.ShapeDtypeStruct((total, rows[0].shape[1]), rows[0].dtype)
    return pl.pallas_call(
        functools.partial(reorder_kernel, (len(rows),)),
        out_shape=(shape,) * len(places),
        grid=(1,),
        in_specs=[pl.BlockSpec(memory_space=pltpu.SMEM)]
        + [pl.BlockSpec(r.shape, lambda i: (0, 0)) for r in rows],
        out_specs=(block,) * len(places),
        compiler_params=pltpu.CompilerParams(vmem_limit_bytes=VMEM_LIMIT),
        name="reorder",
    )(jnp.stack(places), *rows)


def reorder_far_kernel(places, first_in, second_in, far, far_pair, first, second):
    for which, dst in enumerate((first, second)):
        for j in range(32):
            start = pl.multiple_of(places[which, j] * 128, 128)
            dst[:128, j * 128 : (j + 1) * 128] = far[:, pl.ds(start, 128)]
            dst[128:, j * 128 : (j + 1) * 128] = far_pair[:, pl.ds(start, 128)]


def reorder_far(places, first, second, far, far_pair):
    shape = jax.ShapeDtypeStruct(first.shape, first.dtype)
    whole = pl.BlockSpec(memory_space=pl.ANY)
    near = pl.BlockSpec(far.shape, lambda i: (0, 0))
    half = pl.BlockSpec((first.shape[0] // 2, first.shape[1]), lambda i: (1, 0))
    return pl.pallas_call(
        reorder_far_kernel,
        grid=(1,),
        out_shape=(shape, shape),
        in_specs=[pl.BlockSpec(memory_space=pltpu.SMEM), whole, whole, near, near],
        out_specs=(half, half),
        input_output_aliases={1: 0, 2: 1},
        compiler_params=pltpu.CompilerParams(vmem_limit_bytes=VMEM_LIMIT),
        name="reorder_far",
    )(jnp.stack(places), first, second, far, far_pair)


def columns_kernel(slots, rows, stage, rest, out):
    value = rows[...]
    for part in range(8):
        for pair in range(2):
            weights = []
            for i in range(2):
                place = slots[part * 4 + pair * 2 + i]
                inner = place % 16
                weights.append(jnp.where(place // 16 == 0, stage[inner], rest[inner]))
            total = dot_nt(value, jnp.concatenate(weights, 0))
            out[part, :, pair * 256 : (pair + 1) * 256] = total.astype(BF)


def column_parts(slots, rows, stage, rest):
    vmem = pl.BlockSpec(memory_space=pltpu.VMEM)
    return pl.pallas_call(
        columns_kernel,
        out_shape=jax.ShapeDtypeStruct((8, rows.shape[0], 512), BF),
        in_specs=[pl.BlockSpec(memory_space=pltpu.SMEM)] + [vmem] * 3,
        out_specs=vmem,
        compiler_params=pltpu.CompilerParams(vmem_limit_bytes=VMEM_LIMIT),
        name="columns",
    )(slots, rows, stage.reshape(16, 128, -1), rest.reshape(16, 128, -1))


def dot_nt(a, b):
    return lax.dot_general(a, b, (((1,), (1,)), ((), ())), preferred_element_type=F32)


def dot_tn(a, b):
    return lax.dot_general(a, b, (((0,), (0,)), ((), ())), preferred_element_type=F32)


def dot_nn(a, b):
    return jnp.dot(a, b, preferred_element_type=F32)


def attention_kernel(slots, entries, query, d_ctx, *refs):
    near, next_near, far = refs[0:4], refs[4:8], refs[8:12]
    context, d_query = refs[12:14]
    d_near, d_sent = refs[14:18], refs[18:22]
    ctx_f, dq_f = refs[22:24]
    d_far, sems = refs[24:28], refs[28]
    scale = 1.0 / math.sqrt(HS)
    spans = query.shape[0] // CH

    def load(lane, use):
        place = slots[lane, use]
        inner = place % 16
        entry = (inner % 8) * 2 + entries[lane, use]
        mine = jnp.where(inner // 8 == 0, near[lane][entry], next_near[lane][entry])
        return jnp.where(place // 16 == 0, mine, far[lane][inner])

    def store(lane, use, value):
        place = slots[lane, use]
        side, inner = place // 16, place % 16
        d_near[lane][inner] = jnp.where(side == 0, value, d_near[lane][inner])
        d_far[lane][inner] = jnp.where(side == 1, value, d_far[lane][inner])

    heads = range(2)
    for c in range(spans):
        rows = slice(c * CH, (c + 1) * CH)
        uses = (2 * c, 2 * c + 1)
        cols = [slice(h * HS, (h + 1) * HS) for h in heads]
        q = [query[rows, cols[h]] for h in heads]
        dc = [d_ctx[rows, cols[h]] for h in heads]
        keys = [jnp.concatenate([load(h, u) for u in uses], 0) for h in heads]
        values = [jnp.concatenate([load(2 + h, u) for u in uses], 0) for h in heads]
        scores = [dot_nt(q[h], keys[h]) for h in heads]
        d_probs = [dot_nt(dc[h], values[h]) for h in heads]
        raised = [jnp.exp(scores[h] * scale) for h in heads]
        probs = [raised[h] / jnp.sum(raised[h], -1, keepdims=True) for h in heads]
        low = [probs[h].astype(BF) for h in heads]
        row_dot = [jnp.sum(probs[h] * d_probs[h], -1, keepdims=True) for h in heads]
        d_scores = [(probs[h] * (d_probs[h] - row_dot[h])).astype(BF) for h in heads]
        d_values = [dot_tn(low[h], dc[h]).astype(BF) for h in heads]
        d_keys = [(dot_tn(d_scores[h], q[h]) * scale).astype(BF) for h in heads]
        for h in heads:
            ctx_f[rows, cols[h]] = dot_nn(low[h], values[h])
            dq_f[rows, cols[h]] = dot_nn(d_scores[h], keys[h]) * scale
        for h in heads:
            for half, u in enumerate(uses):
                store(h, u, d_keys[h][half * RLEN : (half + 1) * RLEN])
                store(2 + h, u, d_values[h][half * RLEN : (half + 1) * RLEN])
    copies = [pltpu.make_async_copy(d_far[i], d_sent[i], sems.at[i]) for i in range(4)]
    for copy in copies:
        copy.start()
    row = lax.broadcasted_iota(jnp.int32, ctx_f.shape, 0)
    for src, dst in ((ctx_f, context), (dq_f, d_query)):
        moved = pltpu.roll(src[...], CH - 1, 0)
        dst[...] = jnp.where(row >= CH - 1, moved, 0.0).astype(BF)
    for copy in copies:
        copy.wait()


def attention(slots, entries, query, d_ctx, near, next_near, far):
    rows = jax.ShapeDtypeStruct(query.shape, BF)
    part = jax.ShapeDtypeStruct((16, RLEN, HS), BF)
    smem = pl.BlockSpec(memory_space=pltpu.SMEM)
    vmem = pl.BlockSpec(memory_space=pltpu.VMEM)
    ins = [query, d_ctx, *near, *next_near, *far]
    out = pl.pallas_call(
        attention_kernel,
        out_shape=(rows, rows) + (part,) * 8,
        in_specs=[smem, smem] + [vmem] * len(ins),
        out_specs=(vmem,) * 6 + (pl.BlockSpec(memory_space=pltpu.HBM),) * 4,
        scratch_shapes=[pltpu.VMEM(query.shape, F32), pltpu.VMEM(query.shape, F32)]
        + [pltpu.VMEM(part.shape, BF)] * 4
        + [pltpu.SemaphoreType.DMA((4,))],
        compiler_params=pltpu.CompilerParams(vmem_limit_bytes=VMEM_LIMIT),
        name="attention",
    )(slots, entries, *ins)
    return out[0], out[1], out[2:6], out[6:10]


def shift_in(rows):
    filler = jnp.zeros((CH - 1,) + rows.shape[1:], rows.dtype)
    return jnp.concatenate([rows[CH - 1 :], filler], 0)


def on_device(tokens, encoded, neighbour_ids, w_query, w_key, w_value, w_out, d_out):
    me_x, me_y, me_zh = lax.axis_index("x"), lax.axis_index("y"), lax.axis_index("zh")
    me_c = lax.axis_index("c")
    here = (me_zh, me_y, me_x)
    bit = jnp.arange(2, dtype=jnp.int32)
    cols = w_query.shape[1]
    width = tokens.shape[2]
    chunk = width // 32
    names = ("q", "o", "k", "v")
    places = {n: places_of(PATHS[n], *here) for n in names}

    mine = jnp.stack([w_query, w_out.T, w_key, w_value])
    (ids,) = gate((neighbour_ids,), mine)
    wanted = ids[0].reshape(-1)
    their_ids = [trade(wanted, PATHS[n][3]) for n in TABLES]
    other = swap(mine, "zh")
    stage = {n: jnp.stack([mine[i], other[i]]) for i, n in enumerate(names)}
    (encoded,) = gate((encoded,), other)
    for step in range(3):
        came = {n: trade(stage[n], PATHS[n][step]) for n in names}
        if step == 1:
            near_rows, tokens, d_out = gate(
                (encoded.reshape(-1, width), tokens, d_out), *came.values()
            )
        if step >= 1:
            came = dict(zip(names, gate([came[n] for n in names])))
        stage = {n: jnp.stack([stage[n], came[n]]) for n in names}
    stage = {n: stage[n].reshape(width // 2, cols) for n in names}
    rest = {n: trade(stage[n], PATHS[n][3]) for n in names}
    half = width // 2

    asks = jnp.stack([wanted] * 4 + their_ids)
    block, entry = asks // 2, asks % 2
    entries = jnp.where((block // 16) == me_zh, entry, entry ^ me_c)
    slots = jnp.stack([position(PATHS[TABLES[i % 4]], block[i], *here) for i in range(8)])
    hit = slots[:, :, None, None] == jnp.arange(16, dtype=jnp.int32)[:, None]
    hit = hit & (entries[:, :, None, None] == bit)
    asked = jnp.max(hit.astype(jnp.int32), axis=1)
    (asked,) = gate((asked == 1,))
    slots, entries = slots[:4], entries[:4]

    far = swap(encoded[me_c], "zh")
    far_pair = swap(far, "c")
    (tok_q,) = reorder([places["q"]], tokens[0])
    (up_o,) = reorder([places["o"]], d_out[0])
    kv_places = [places["k"], places["v"]]
    enc_k, enc_v = reorder(kv_places, near_rows, total=2 * near_rows.shape[0])
    enc_k, enc_v = reorder_far(kv_places, enc_k, enc_v, far, far_pair)

    def project(rows, name):
        first = dot_nn(rows[:, :half], stage[name])
        return (first + dot_nn(rows[:, half:], rest[name])).astype(BF)

    keys, values = project(enc_k, "k"), project(enc_v, "v")
    query, d_context = shift_in(project(tok_q, "q")), shift_in(project(up_o, "o"))
    tables = [
        t.reshape(2, 2, RLEN, HS)
        for t in (keys[:, :HS], keys[:, HS:], values[:, :HS], values[:, HS:])
    ]
    for step in range(3):
        came = [trade(t, PATHS[n][step]) for t, n in zip(tables, TABLES)]
        if step < 2:
            tables = [jnp.stack([t, r]) for t, r in zip(tables, came)]
    near = [t.reshape(16, RLEN, HS) for t in tables]
    next_near = [t.reshape(16, RLEN, HS) for t in came]

    def choose(lane):
        parts = []
        for i, t in enumerate((near[lane], next_near[lane])):
            pairs = t.reshape(8, 2, RLEN, HS)
            second = asked[4 + lane, 8 * i : 8 * (i + 1), 1][:, None, None]
            parts.append(jnp.where(second, pairs[:, 1], pairs[:, 0]))
        return jnp.concatenate(parts, 0)

    far_side = [trade(choose(i), PATHS[n][3]) for i, n in enumerate(TABLES)]
    context, d_query, d_near, d_far = attention(
        slots, entries, query, d_context, near, next_near, far_side
    )

    numbers = jnp.arange(32, dtype=jnp.int32)

    def group_sum(rows, name):
        parts = column_parts(position(PATHS[name], numbers, *here), rows, stage[name], rest[name])
        return lax.psum_scatter(parts, ("zl", "c"), scatter_dimension=0, tiled=False)


    back = [trade(t, PATHS[n][3]) for t, n in zip(d_far, TABLES)]

    out_rows, dx_rows = gate((context, d_query), *back)
    attended, d_tokens = group_sum(out_rows, "o"), group_sum(dx_rows, "q")

    def by_entry(lane, rows):
        own, came = d_near[lane][rows].astype(F32), back[lane][rows].astype(F32)
        total = []
        for e in range(2):
            ours = asked[lane, rows, e][:, None, None]
            theirs = asked[4 + lane, rows, e][:, None, None]
            total.append(jnp.where(ours, own, 0.0) + jnp.where(theirs, came, 0.0))
        return jnp.stack(total, 1).astype(BF)

    sums = []
    for lane in range(4):
        sums.append((by_entry(lane, slice(0, 8)), by_entry(lane, slice(8, 16))))
    for step in (2, 1, 0):
        sent = [s[1] for s in sums]
        came = [trade(s, PATHS[n][step]) for s, n in zip(sent, TABLES)]
        h = sent[0].shape[0] // 2
        if step == 0:
            sums = [add_low(s[0], r) for s, r in zip(sums, came)]
        else:
            sums = [
                (add_low(s[0][:h], r[:h]), add_low(s[0][h:], r[h:])) for s, r in zip(sums, came)
            ]
    rows = 4 * RLEN
    sums = [s.reshape(rows, HS) for s in sums]
    entry_k = jnp.concatenate(sums[:2], 1)
    entry_v = jnp.concatenate(sums[2:], 1)

    def halves(rows_in, grads):
        return (
            dot_tn(rows_in[:, :half], grads).astype(BF),
            dot_tn(rows_in[:, half:], grads).astype(BF),
        )

    def block_sum(terms, name, gates=(None,) * 4):
        keep, send = terms
        for step, wait in zip((3, 2, 1, 0), gates):
            if wait is not None:
                (send,) = gate((send,), wait)
            came = trade(send, PATHS[name][step])
            if step == 0:
                return add_low(keep, came)
            h = keep.shape[0] // 2
            keep, send = add_low(keep[:h], came[:h]), add_low(keep[h:], came[h:])

    def z_sum(a, b, *after):
        ours = [t.reshape(2, chunk, cols) for t in (a, b)]
        send = jnp.stack([t[1] for t in ours])
        if after:
            (send,) = gate((send,), *after)
        came = swap(send, "zh")
        return [t[0].astype(F32) + came[i].astype(F32) for i, t in enumerate(ours)]

    tok_q, up_o = gate((tok_q, up_o), *sums)
    sum_q = block_sum(halves(tok_q, d_query), "q")
    sum_o = block_sum(halves(up_o, context), "o")
    grad_query, grad_out = z_sum(sum_q, sum_o)
    sum_k = block_sum(halves(enc_k, entry_k), "k")
    sum_v = block_sum(halves(enc_v, entry_v), "v")
    grad_key, grad_value = z_sum(sum_k, sum_v)

    return attended[None], d_tokens[None], grad_query, grad_key, grad_value, grad_out.T


def solution(mesh):
    grid = Mesh(mesh.devices.reshape(4, 2, 2, 4, 4), ("zl", "c", "zh", "y", "x"))
    grp, nbr = ("zl", "c"), ("zh", "y", "x")
    in_specs = (
        P(nbr, None, None),
        P(nbr, None, None),
        P(nbr, None, None),
        P(nbr, grp),
        P(nbr, grp),
        P(nbr, grp),
        P(grp, nbr),
        P(nbr, None, None),
    )
    out_specs = (
        P(nbr, None, grp),
        P(nbr, None, grp),
        P(nbr, grp),
        P(nbr, grp),
        P(nbr, grp),
        P(grp, nbr),
    )
    return jax.shard_map(
        on_device, mesh=grid, in_specs=in_specs, out_specs=out_specs, check_vma=False
    )
```
